128 devices in a mesh: dp: 16 (over y, x_lo, core), blk: 8 (over z, x_hi).
Axes of the slice: x: 4 (x_hi: 2, x_lo: 2; x = x_hi * 2 + x_lo), y: 4, z: 4, core: 2. Of those that a mesh axis runs over, the one named last changes fastest.
Arguments:
- tokens: bfloat16 [8, 512, 5120], P('blk'), may hold values from -6 to 6
- cotangent: bfloat16 [8, 512, 5120], P('blk'), may hold values from -0.119628906 to 0.119628906
- gain: float32 [5120], replicated, may hold values from 0.1 to 1.9
- up_weight: bfloat16 [13824, 5120], P(('dp', 'blk')), may hold values from -0.078125 to 0.078125
- down_weight: bfloat16 [13824, 5120], P(('dp', 'blk')), may hold values from -0.0546875 to 0.0546875
Outputs:
- block_out: bfloat16 [8, 512, 5120], P('blk', 'dp')
- grad_gain: float32 [5120], replicated
- grad_up: bfloat16 [13824, 5120], P(('dp', 'blk'))
- grad_down: bfloat16 [13824, 5120], P(('dp', 'blk'))
The draws below stay inside these ranges and needn't reach their ends.
All inputs are finite; a program needn't handle non-finite values.
Results may differ from the reference program's by a relative error of at most 0.017.
Values may be sent and summed in bfloat16 or wider, within the bound.
A program may use at most 192 MiB of HBM per device.

```python
import jax
import jax.numpy as jnp
from jax import lax

D = 5120
FF = 13824
TOK = 512
MICRO = 8
N_DP = 16


def block_scale(own_key, extent, split, least, high):
    level = 1.0
    for axis_at, blocks in split:
        draws = jax.random.uniform(jax.random.fold_in(jax.random.fold_in(own_key, 6), axis_at), (blocks,), jnp.float32, least / len(split), high / len(split))
        level = level * jnp.repeat(jnp.exp(draws), extent[axis_at] // blocks).reshape((-1,) + (1,) * (len(extent) - 1 - axis_at))
    return level


def normal_values(rng, shape, spread, limit, pieces=(), kind=jnp.bfloat16):
    array = jax.random.normal(rng, shape, jnp.float32) * spread
    if len(pieces) > 0:
        array = block_scale(rng, shape, pieces, -0.22, 0.18) * array
    return jnp.clip(array, min=-limit, max=limit).astype(kind)


def setup_inputs(seed: int = 0) -> dict:
    splits = jax.random.split(jax.random.key(seed), 6)
    tokens = normal_values(splits[0], (MICRO, TOK, D), 1.0, 6.0, ((0, 8),))
    cotangent = normal_values(splits[1], (MICRO, TOK, D), 0.02, 0.119628906, ((0, 8),))
    gain = jnp.clip(1.0 + 0.18 * jax.random.normal(splits[2], (D,), jnp.float32), 0.1, 1.9)
    up_weight = normal_values(splits[3], (FF, D), D ** -0.5, 0.078125, ((0, 128),))
    down_weight = normal_values(splits[4], (FF, D), FF ** -0.5, 0.0546875, ((0, 128),))
    return dict(tokens=tokens, cotangent=cotangent, gain=gain, up_weight=up_weight, down_weight=down_weight)


def reference(tokens, cotangent, gain, up_weight, down_weight):
    inputs = tokens.reshape(MICRO * TOK, D).astype(jnp.float32)
    inverse_rms = lax.rsqrt(lax.optimization_barrier(jnp.mean(inputs * inputs, axis=-1, keepdims=True)) + 1e-05)
    unit_rows = inputs * inverse_rms
    normed = (unit_rows * gain).astype(jnp.bfloat16)
    hidden = jnp.dot(normed, up_weight.T, preferred_element_type=jnp.float32)
    active = jax.nn.silu(hidden).astype(jnp.bfloat16)
    group_size = FF // N_DP

    def add_group(total, group):
        act_block = lax.dynamic_slice_in_dim(active, group * group_size, group_size, 1)
        weight_block = lax.dynamic_slice_in_dim(down_weight, group * group_size, group_size, 0)
        term = jnp.dot(act_block, weight_block, preferred_element_type=jnp.float32)
        rounded = lax.optimization_barrier(term.astype(jnp.bfloat16))
        return (total + rounded.astype(jnp.float32), None)
    summed, _ = lax.scan(add_group, jnp.zeros((MICRO * TOK, D), jnp.float32), jnp.arange(N_DP, dtype=jnp.int32))
    block_out = (inputs + summed).astype(jnp.bfloat16).reshape(MICRO, TOK, D)
    upstream = cotangent.reshape(MICRO * TOK, D)
    back_grad = jnp.dot(upstream, down_weight.T, preferred_element_type=jnp.float32)
    sigmoid_h = jax.nn.sigmoid(hidden)
    hidden_grad = (back_grad * sigmoid_h * (1.0 + hidden * (1.0 - sigmoid_h))).astype(jnp.bfloat16)
    normal_grad = jnp.dot(hidden_grad, up_weight, preferred_element_type=jnp.float32)
    grad_gain = lax.optimization_barrier(jnp.sum(normal_grad * unit_rows, axis=0))

    def add_micro(totals, micro):
        first_row = micro * TOK
        grad_rows = lax.dynamic_slice_in_dim(hidden_grad, first_row, TOK, 0)
        norm_rows = lax.dynamic_slice_in_dim(normed, first_row, TOK, 0)
        act_rows = lax.dynamic_slice_in_dim(active, first_row, TOK, 0)
        cot_rows = lax.dynamic_slice_in_dim(upstream, first_row, TOK, 0)
        up_term = jnp.dot(grad_rows.T, norm_rows, preferred_element_type=jnp.float32)
        down_term = jnp.dot(act_rows.T, cot_rows, preferred_element_type=jnp.float32)
        up_round = lax.optimization_barrier(up_term.astype(jnp.bfloat16))
        down_round = lax.optimization_barrier(down_term.astype(jnp.bfloat16))
        return ((totals[0] + up_round.astype(jnp.float32), totals[1] + down_round.astype(jnp.float32)), None)
    empty = jnp.zeros((FF, D), jnp.float32)
    sums, _ = lax.scan(add_micro, (empty, empty), jnp.arange(MICRO, dtype=jnp.int32))
    return (block_out, grad_gain, sums[0].astype(jnp.bfloat16), sums[1].astype(jnp.bfloat16))
```

```python
import jax
import jax.numpy as jnp
from jax import lax
from jax.experimental import pallas as pl
from jax.experimental.pallas import tpu as pltpu
from jax.sharding import PartitionSpec as P

D = 5120
TOK = 512
OWN = 108
SENT = 112
PAD = 128
STEP = 512
HALF = D // 2
HALVES = ((0, HALF), (HALF, D))
MESH = pl.DeviceIdType.MESH
BF16 = jnp.bfloat16
F32 = jnp.float32


def columns(step, size=STEP):
    return pl.ds(pl.multiple_of(step * size, size), size)


def dot(a, b, over):
    return lax.dot_general(a, b, ((over[:1], over[1:]), ((), ())), preferred_element_type=F32)


def kernel(
    tokens_ref, cotangent_ref, gain_ref, up_ref, down_ref,
    out_ref, gain_out_ref, grad_up_ref, grad_down_ref,
    norm, cot, weights, act, act_t, hidden_t, acc, grads, mail, x_first, y_first, y_second, x_second,
    own_rows, gain_acc, gain_own, gain_slots, send_sem, recv_sem, local_sem, free_sem,
):
    dp, blk = lax.axis_index("dp"), lax.axis_index("blk")
    y, x_lo, core = dp // 4, (dp // 2) % 2, dp % 2
    z, x_hi = blk // 2, blk % 2
    x = 2 * x_hi + x_lo

    def chip(cx, cy, cz, cc):
        return (cy * 4 + (cx % 2) * 2 + cc, cz * 2 + cx // 2)

    def x_at(j):
        return chip((x + j) % 4, y, z, core)

    def y_at(j):
        return chip(x, (y + j) % 4, z, core)

    def z_at(j):
        return chip(x, y, (z + j) % 4, core)

    sibling = chip(x, y, z, 1 - core)
    across = chip(3 - x, y, z, core)
    beside = chip(x + 1 - 2 * x_lo, y, z, core)

    count = [0]

    def send(src, dst, device):
        at = count[0]
        count[0] += 1
        copy = pltpu.make_async_remote_copy(
            src_ref=src, dst_ref=dst, send_sem=send_sem.at[at], recv_sem=recv_sem.at[at], device_id=device, device_id_type=MESH
        )
        copy.start()
        return copy

    load_tokens = pltpu.make_async_copy(tokens_ref.at[0], norm.at[0], local_sem.at[0])
    load_cot = pltpu.make_async_copy(cotangent_ref.at[0], cot.at[0], local_sem.at[1])
    load_own = pltpu.make_async_copy(tokens_ref.at[0, y, x_lo, core], own_rows, local_sem.at[2])
    load_tokens.start()
    load_cot.start()
    load_own.start()

    partners = [x_at(1), x_at(2), x_at(3), y_at(1), y_at(2), y_at(3), z_at(1), z_at(2), z_at(3), sibling]
    barrier = pltpu.get_barrier_semaphore()
    for partner in partners:
        pl.semaphore_signal(barrier, inc=1, device_id=partner, device_id_type=MESH)

    for kind, ref in enumerate((up_ref, down_ref)):
        weights[kind, 0, 96:PAD, :] = jnp.zeros((PAD - 96, D), BF16)
        weights[kind, 0, 0:OWN, :] = ref[...]
        for slot in range(1, 4):
            weights[kind, slot, SENT:PAD, :] = jnp.zeros((PAD - SENT, D), BF16)
    pl.semaphore_wait(barrier, len(partners))

    def block(kind, slot):
        return weights.at[kind, slot, pl.ds(0, SENT)]

    up_right = send(block(0, 0), block(0, 2), z_at(1))
    down_left = send(block(1, 0), block(1, 1), z_at(3))
    down_right = send(block(1, 0), block(1, 2), z_at(1))
    up_left = send(block(0, 0), block(0, 1), z_at(3))

    quarter = (y + 2 * x_lo) % 4
    quarter_across = (y + 2 - 2 * x_lo) % 4

    def piece(ref, which, q):
        return ref.at[which, q, :, core]

    load_cot.wait()
    cot_across = send(piece(cot, 0, quarter_across), piece(cot, 1, quarter_across), across)

    load_tokens.wait()
    gain = gain_ref[...]

    def normalize(step, _):
        at = (0, step // 8, (step // 4) % 2, (step // 2) % 2, pl.ds(pl.multiple_of((step % 2) * 16, 16), 16))
        rows = norm[at].astype(F32)
        inverse = lax.rsqrt(jnp.mean(rows * rows, axis=-1, keepdims=True) + 1e-05)
        norm[at] = (rows * inverse * gain).astype(BF16)
        return 0

    lax.fori_loop(0, 32, normalize, 0)
    norm_across = send(piece(norm, 0, quarter_across), piece(norm, 1, quarter_across), across)

    def forward(slot, blocks, m):
        width = blocks * PAD
        acc[...] = jnp.zeros_like(acc)

        def add(step, _):
            at = columns(step)
            for kind, rows in enumerate((norm, cot)):
                left = rows[m, :, :, :, :, at].reshape(TOK, STEP)
                right = weights[kind, slot : slot + blocks, :, at].reshape(width, STEP)
                acc[kind, :, 0:width] += dot(left, right, (1, 1))
            return 0

        lax.fori_loop(0, D // STEP, add, 0)

        def finish(step, _):
            rows = columns(step, 128)
            hidden, back = acc[0, rows, 0:width], acc[1, rows, 0:width]
            sig = 1.0 / (1.0 + jnp.exp(-hidden))
            active = hidden * sig
            hidden_grad = back * sig * (1.0 + hidden * (1.0 - sig))
            to = pl.ds(pl.multiple_of(m * TOK + step * 128, 128), 128)
            act[to, slot * PAD : slot * PAD + width] = active.astype(BF16)
            act_t[slot * PAD : slot * PAD + width, to] = active.T.astype(BF16)
            hidden_t[slot * PAD : slot * PAD + width, to] = hidden_grad.T.astype(BF16)
            return 0

        lax.fori_loop(0, TOK // 128, finish, 0)

    def backward(slot, blocks, first, last):
        rows = pl.ds(slot * PAD, blocks * PAD)

        def tile(step, _):
            at = columns(step)
            up_part = dot(hidden_t[rows, :], norm[:, :, :, :, :, at].reshape(2 * TOK, STEP), (1, 0))
            terms = weights[0, slot : slot + blocks, :, at].reshape(blocks * PAD, STEP).astype(F32) * up_part
            gain_acc[:, at] += jnp.sum(terms.reshape(blocks * PAD // 8, 8, STEP), axis=0)
            down_part = dot(act_t[rows, :], cot[:, :, :, :, :, at].reshape(2 * TOK, STEP), (1, 0))
            for b in range(blocks):
                grads[0, slot + b, :, at] = up_part[b * PAD : b * PAD + SENT].astype(BF16)
                grads[1, slot + b, :, at] = down_part[b * PAD : b * PAD + SENT].astype(BF16)
            return 0

        lax.fori_loop(first // STEP, last // STEP, tile, 0)

    gain_acc[...] = jnp.zeros_like(gain_acc)
    forward(0, 1, 0)

    onward = []
    for ref, copy in ((cot, cot_across), (norm, norm_across)):
        copy.wait_recv()
        src = piece(ref, 1, quarter)
        onward.append([send(src, src, device) for device in (beside, y_at(1), y_at(3))] + [send(src, src, sibling)])
    up_right.wait_recv()
    up_relay = send(block(0, 2), block(0, 3), z_at(1))
    down_left.wait_recv()
    down_relay = send(block(1, 1), block(1, 3), z_at(3))
    shared = []
    for ref, copies in ((cot, onward[0]), (norm, onward[1])):
        for shift, copy in ((2, copies[0]), (3, copies[1]), (1, copies[2])):
            copy.wait_recv()
            src = piece(ref, 1, (quarter + shift) % 4)
            shared.append(send(src, src, sibling))
    for copy in [onward[0][3], onward[1][3]] + shared:
        copy.wait_recv()

    forward(0, 1, 1)
    down_right.wait_recv()
    up_left.wait_recv()

    def forward_pair(m, _):
        forward(1, 2, m)
        return 0

    lax.fori_loop(0, 2, forward_pair, 0)

    direct = []
    for first, last in HALVES:
        backward(0, 3, first, last)
        at = pl.ds(first, HALF)
        direct.append(
            (
                send(grads.at[1, 1, :, at], mail.at[1, 0, :, at], z_at(1)),
                send(grads.at[0, 2, :, at], mail.at[0, 0, :, at], z_at(3)),
            )
        )

    up_relay.wait_recv()
    down_relay.wait_recv()

    def forward_far(m, _):
        forward(3, 1, m)
        return 0

    lax.fori_loop(0, 2, forward_far, 0)
    far = []
    for first, last in HALVES:
        backward(3, 1, first, last)
        at = pl.ds(first, HALF)
        far.append(
            (
                send(grads.at[0, 3, :, at], mail.at[0, 1, :, at], z_at(1)),
                send(grads.at[1, 3, :, at], mail.at[1, 1, :, at], z_at(3)),
            )
        )

    for copy in [cot_across, norm_across] + onward[0] + onward[1] + shared:
        copy.wait_send()
    pl.semaphore_signal(free_sem, inc=1, device_id=sibling, device_id_type=MESH)
    gain_own[...] = jnp.sum(gain_acc[...], axis=0, keepdims=True)
    gain_core = send(gain_own, gain_slots.at[0, 0], sibling)

    def project(first, last):
        def tile(step, _):
            at = columns(step)
            right = weights[1, :, :, at].reshape(4 * PAD, STEP)
            for m in range(2):
                part = dot(act[m * TOK : (m + 1) * TOK, :], right, (1, 0))
                norm[m, :, :, :, :, at] = part.astype(BF16).reshape(4, 2, 2, 32, STEP)
            return 0

        lax.fori_loop(first // STEP, last // STEP, tile, 0)

    halves = []
    for first, last in HALVES:
        project(first, last)
        if first == 0:
            pl.semaphore_wait(free_sem, 1)
        at = pl.ds(first, HALF)
        halves.append(send(norm.at[:, :, :, 1 - core, :, at], cot.at[:, :, :, 0, :, at], sibling))

    def add_core(first):
        def tile(step, _):
            at = (step // 8, (step // 2) % 4, step % 2)
            cols = pl.ds(first, HALF)
            mine = norm[(*at, core, slice(None), cols)].astype(F32)
            theirs = cot[(*at, 0, slice(None), cols)].astype(F32)
            cot[(*at, 0, slice(None), cols)] = (mine + theirs).astype(BF16)
            return 0

        lax.fori_loop(0, 16, tile, 0)

    def microbatch(cx):
        return (cx // 2 + x_hi) % 2

    left, right = pl.ds(0, HALF), pl.ds(HALF, HALF)
    halves[0].wait_recv()
    add_core(0)
    along_x = []
    for j in range(1, 4):
        to = (x + j) % 4
        along_x.append(send(cot.at[microbatch(to), :, to % 2, 0, :, left], x_first.at[j - 1], x_at(j)))
    halves[1].wait_recv()
    add_core(HALF)
    along_y = []
    for j in range(1, 4):
        along_y.append(send(cot.at[:, (y + j) % 4, :, 0, :, right], y_first.at[j - 1], y_at(j)))

    def spread(stage, place, others):
        gain_slots[stage, place] = gain_own[...]
        return [send(gain_own, gain_slots.at[stage, place], other) for other in others]

    def gather(stage, copies):
        for copy in copies:
            copy.wait()
        gain_own[...] = (gain_slots[stage, 0] + gain_slots[stage, 1]) + (gain_slots[stage, 2] + gain_slots[stage, 3])

    gain_core.wait()
    gain_own[...] = gain_own[...] + gain_slots[0, 0]
    gain_x = spread(1, x, [x_at(j) for j in range(1, 4)])

    last_leg = []
    for half, (first, last) in enumerate(HALVES):
        at = pl.ds(first, HALF)
        for copy in far[half]:
            copy.wait_recv()

        def combine(step, _):
            cols = columns(step)
            grads[0, 1, :, cols] = (grads[0, 1, :, cols].astype(F32) + mail[0, 1, :, cols].astype(F32)).astype(BF16)
            grads[1, 2, :, cols] = (grads[1, 2, :, cols].astype(F32) + mail[1, 1, :, cols].astype(F32)).astype(BF16)
            return 0

        lax.fori_loop(first // STEP, last // STEP, combine, 0)
        last_leg.append(
            (
                send(grads.at[0, 1, :, at], mail.at[0, 2, :, at], z_at(1)),
                send(grads.at[1, 2, :, at], mail.at[1, 2, :, at], z_at(3)),
            )
        )
        if half == 0:
            gather(1, gain_x)
            gain_y = spread(2, y, [y_at(j) for j in range(1, 4)])

    gather(2, gain_y)
    gain_z = spread(3, z, [z_at(j) for j in range(1, 4)])

    for copy in along_x:
        copy.wait()

    def add_x(step, _):
        total = cot[0, step, x_lo, 0, :, left].astype(F32)
        for j in range(3):
            total += x_first[j, step].astype(F32)
        x_first[0, step] = total.astype(BF16)
        return 0

    lax.fori_loop(0, 4, add_x, 0)
    then_y = [send(x_first.at[0, (y + j) % 4], y_second.at[j - 1], y_at(j)) for j in range(1, 4)]
    for copy in along_y:
        copy.wait()

    def add_y(step, _):
        at = (step // 2, step % 2)
        total = cot[(at[0], y, at[1], 0, slice(None), right)].astype(F32)
        for j in range(3):
            total += y_first[(j, *at)].astype(F32)
        y_first[(0, *at)] = total.astype(BF16)
        return 0

    lax.fori_loop(0, 4, add_y, 0)
    then_x = []
    for j in range(1, 4):
        to = (x + j) % 4
        then_x.append(send(y_first.at[0, microbatch(to), to % 2], x_second.at[j - 1], x_at(j)))

    load_own.wait()
    gather(3, gain_z)
    gain_out_ref[...] = gain_own[...] / gain
    for copy in then_y:
        copy.wait()
    total = own_rows[:, left].astype(F32) + x_first[0, y].astype(F32)
    for j in range(3):
        total += y_second[j].astype(F32)
    out_ref[:, left] = total.astype(BF16)
    for copy in then_x:
        copy.wait()
    total = own_rows[:, right].astype(F32) + y_first[0, 0, x_lo].astype(F32)
    for j in range(3):
        total += x_second[j].astype(F32)
    out_ref[:, right] = total.astype(BF16)

    for half, (first, last) in enumerate(HALVES):
        for copy in (*direct[half], *last_leg[half]):
            copy.wait_recv()

        def finish(step, _):
            cols = columns(step)
            for kind, ref in enumerate((grad_up_ref, grad_down_ref)):
                total = grads[kind, 0, :, cols].astype(F32)
                total += mail[kind, 0, :, cols].astype(F32)
                total += mail[kind, 2, :, cols].astype(F32)
                ref[:, cols] = total[0:OWN].astype(BF16)
            return 0

        lax.fori_loop(first // STEP, last // STEP, finish, 0)

    for copy in [up_right, down_left, down_right, up_left, up_relay, down_relay, *halves]:
        copy.wait_send()
    for pairs in (direct, far, last_leg):
        for pair in pairs:
            for copy in pair:
                copy.wait_send()


COPIES = 64


def body(tokens, cotangent, gain, up_weight, down_weight):
    vmem, anywhere = pl.BlockSpec(memory_space=pltpu.VMEM), pl.BlockSpec(memory_space=pl.ANY)
    rows = (1, 4, 2, 2, 32, D)
    out, gain_out, grad_up, grad_down = pl.pallas_call(
        kernel,
        out_shape=(
            jax.ShapeDtypeStruct((32, D), BF16),
            jax.ShapeDtypeStruct((1, D), F32),
            jax.ShapeDtypeStruct((OWN, D), BF16),
            jax.ShapeDtypeStruct((OWN, D), BF16),
        ),
        in_specs=[anywhere, anywhere, vmem, vmem, vmem],
        out_specs=(vmem, vmem, vmem, vmem),
        scratch_shapes=[
            pltpu.VMEM((2, 4, 2, 2, 32, D), BF16),
            pltpu.VMEM((2, 4, 2, 2, 32, D), BF16),
            pltpu.VMEM((2, 4, PAD, D), BF16),
            pltpu.VMEM((2 * TOK, 4 * PAD), BF16),
            pltpu.VMEM((4 * PAD, 2 * TOK), BF16),
            pltpu.VMEM((4 * PAD, 2 * TOK), BF16),
            pltpu.VMEM((2, TOK, 2 * PAD), F32),
            pltpu.VMEM((2, 4, SENT, D), BF16),
            pltpu.VMEM((2, 3, SENT, D), BF16),
            pltpu.VMEM((3, 4, 32, HALF), BF16),
            pltpu.VMEM((3, 2, 2, 32, HALF), BF16),
            pltpu.VMEM((3, 32, HALF), BF16),
            pltpu.VMEM((3, 32, HALF), BF16),
            pltpu.VMEM((32, D), BF16),
            pltpu.VMEM((8, D), F32),
            pltpu.VMEM((1, D), F32),
            pltpu.VMEM((4, 4, 1, D), F32),
            pltpu.SemaphoreType.DMA((COPIES,)),
            pltpu.SemaphoreType.DMA((COPIES,)),
            pltpu.SemaphoreType.DMA((3,)),
            pltpu.SemaphoreType.REGULAR,
        ],
        compiler_params=pltpu.CompilerParams(collective_id=0, has_side_effects=True, vmem_limit_bytes=63 * 2**20),
    )(tokens.reshape(rows), cotangent.reshape(rows), gain[None], up_weight, down_weight)
    return (out[None], gain_out[0], grad_up, grad_down)


def solution(mesh):
    placed = (
        P("blk", None, None),
        P("blk", None, None),
        P(),
        P(("dp", "blk"), None),
        P(("dp", "blk"), None),
    )
    return jax.shard_map(
        body,
        mesh=mesh,
        in_specs=placed,
        out_specs=(P("blk", "dp", None), P(), P(("dp", "blk"), None), P(("dp", "blk"), None)),
        check_vma=False,
    )
```

```python
import jax
import jax.numpy as jnp
from jax import lax
from jax.experimental import pallas as pl
from jax.experimental.pallas import tpu as pltpu
from jax.sharding import PartitionSpec as P

D = 5120
TOK = 512
OWN = 108
MAIN = 96
PAD = 128
STEP = 256
HALF = D // 2
FOURTH = D // 4
TAIL = 3 * FOURTH
MESH = pl.DeviceIdType.MESH
BF16 = jnp.bfloat16
F32 = jnp.float32


def columns(step, size=STEP, first=0):
    return pl.ds(pl.multiple_of(first + step * size, size), size)


def row_numbers(like):
    return lax.broadcasted_iota(jnp.int32, like.shape, 0)


def pack(fourth, last, at):
    return jnp.where(row_numbers(fourth) < 12, fourth, pltpu.roll(last, 12 - 4 * at, 0))


def unpack(fourths):
    row = row_numbers(fourths[0])
    moved = [pltpu.roll(fourth, 4 * at + 4, 0) for at, fourth in enumerate(fourths)]
    last = jnp.where(row < 4, moved[0], jnp.where(row < 8, moved[1], jnp.where(row < 12, moved[2], 0.0)))
    return [jnp.where(row < 12, fourth, 0.0) for fourth in fourths] + [last]


def dot(a, b, over):
    return lax.dot_general(a, b, ((over[:1], over[1:]), ((), ())), preferred_element_type=F32)


def kernel(
    tokens_ref, cotangent_ref, gain_ref, up_ref, down_ref,
    out_ref, gain_out_ref, grad_up_ref, grad_down_ref,
    norm, cot, weights, tails, act, act_t, hidden_t, acc, grads, grad_tails, mail, mail_tails,
    x_first, y_first, y_second, x_second,
    own_rows, gain_acc, gain_own, gain_slots, send_sem, recv_sem, local_sem, free_sem,
):
    dp, blk = lax.axis_index("dp"), lax.axis_index("blk")
    y, x_lo, core = dp // 4, (dp // 2) % 2, dp % 2
    z, x_hi = blk // 2, blk % 2
    x = 2 * x_hi + x_lo

    def chip(cx, cy, cz, cc):
        return (cy * 4 + (cx % 2) * 2 + cc, cz * 2 + cx // 2)

    def x_at(j):
        return chip((x + j) % 4, y, z, core)

    def y_at(j):
        return chip(x, (y + j) % 4, z, core)

    def z_at(j):
        return chip(x, y, (z + j) % 4, core)

    sibling = chip(x, y, z, 1 - core)
    across = chip(3 - x, y, z, core)
    beside = chip(x + 1 - 2 * x_lo, y, z, core)

    count = [0]

    def send(src, dst, device):
        at = count[0]
        count[0] += 1
        copy = pltpu.make_async_remote_copy(
            src_ref=src, dst_ref=dst, send_sem=send_sem.at[at], recv_sem=recv_sem.at[at], device_id=device, device_id_type=MESH
        )
        copy.start()
        return copy

    load_tokens = pltpu.make_async_copy(tokens_ref.at[0], norm.at[0], local_sem.at[0])
    load_cot = pltpu.make_async_copy(cotangent_ref.at[0], cot.at[0], local_sem.at[1])
    load_own = pltpu.make_async_copy(tokens_ref.at[0, y, x_lo, core], own_rows, local_sem.at[2])
    load_tokens.start()
    load_cot.start()
    load_own.start()

    partners = [x_at(1), x_at(2), x_at(3), y_at(1), y_at(2), y_at(3), z_at(1), z_at(2), z_at(3), sibling]
    barrier = pltpu.get_barrier_semaphore()
    for partner in partners:
        pl.semaphore_signal(barrier, inc=1, device_id=partner, device_id_type=MESH)

    def fourth_of(at):
        return pl.ds(at * FOURTH, FOURTH)

    for kind, ref in enumerate((up_ref, down_ref)):
        weights[kind, 0, MAIN:PAD, :] = jnp.zeros((PAD - MAIN, D), BF16)
        weights[kind, 0, 0:OWN, :] = ref[...]
        last = weights[kind, 0, MAIN : MAIN + 16, fourth_of(3)].astype(F32)
        for at in range(3):
            rows = weights[kind, 0, MAIN : MAIN + 16, fourth_of(at)].astype(F32)
            tails[kind, 0, :, fourth_of(at)] = pack(rows, last, at).astype(BF16)
        for slot in range(1, 4):
            weights[kind, slot, MAIN + 16 : PAD, :] = jnp.zeros((PAD - MAIN - 16, D), BF16)
    pl.semaphore_wait(barrier, len(partners))

    def send_block(kind, slot, to, device):
        return [
            send(weights.at[kind, slot, pl.ds(0, MAIN)], weights.at[kind, to, pl.ds(0, MAIN)], device),
            send(tails.at[kind, slot], tails.at[kind, to], device),
        ]

    def wait_recv(copies):
        for copy in copies:
            copy.wait_recv()

    def unpack_block(kind, slot):
        fourths = unpack([tails[kind, slot, :, fourth_of(at)].astype(F32) for at in range(3)])
        for at in range(4):
            weights[kind, slot, MAIN : MAIN + 16, fourth_of(at)] = fourths[at].astype(BF16)

    up_right = send_block(0, 0, 2, z_at(1))
    down_left = send_block(1, 0, 1, z_at(3))
    down_right = send_block(1, 0, 2, z_at(1))
    up_left = send_block(0, 0, 1, z_at(3))

    quarter = (y + 2 * x_lo) % 4
    quarter_across = (y + 2 - 2 * x_lo) % 4

    def piece(ref, which, q):
        return ref.at[which, q, :, core]

    load_cot.wait()
    cot_across = send(piece(cot, 0, quarter_across), piece(cot, 1, quarter_across), across)

    load_tokens.wait()
    gain = gain_ref[...]

    def normalize(step, _):
        at = (0, step // 8, (step // 4) % 2, (step // 2) % 2, pl.ds(pl.multiple_of((step % 2) * 16, 16), 16))
        rows = norm[at].astype(F32)
        inverse = lax.rsqrt(jnp.mean(rows * rows, axis=-1, keepdims=True) + 1e-05)
        norm[at] = (rows * inverse * gain).astype(BF16)
        return 0

    lax.fori_loop(0, 32, normalize, 0)
    norm_across = send(piece(norm, 0, quarter_across), piece(norm, 1, quarter_across), across)

    def forward(slot, blocks, micros):
        width = blocks * PAD
        tall = len(micros) * TOK
        first_row = micros[0] * TOK
        which = slice(micros[0], micros[0] + len(micros))

        for kind, rows in enumerate((norm, cot)):
            left = rows[which].reshape(tall, D)
            right = weights[kind, slot : slot + blocks].reshape(width, D)
            acc[kind, 0:tall, 0:width] = dot(left, right, (1, 1))

        def finish(step, _):
            rows = columns(step, 128)
            hidden, back = acc[0, rows, 0:width], acc[1, rows, 0:width]
            sig = 1.0 / (1.0 + jnp.exp(-hidden))
            active = hidden * sig
            hidden_grad = back * sig * (1.0 + hidden * (1.0 - sig))
            to = columns(step, 128, first_row)
            act[to, slot * PAD : slot * PAD + width] = active.astype(BF16)
            act_t[slot * PAD : slot * PAD + width, to] = active.T.astype(BF16)
            hidden_t[slot * PAD : slot * PAD + width, to] = hidden_grad.T.astype(BF16)
            return 0

        lax.fori_loop(0, tall // 128, finish, 0)

    def backward(slot, blocks, fourth):
        rows = pl.ds(slot * PAD, blocks * PAD)

        at = fourth_of(fourth)
        up_part = dot(hidden_t[rows, :], norm[:, :, :, :, :, at].reshape(2 * TOK, FOURTH), (1, 0))
        terms = weights[0, slot : slot + blocks, :, at].reshape(blocks * PAD, FOURTH).astype(F32) * up_part
        gain_acc[:, at] += jnp.sum(terms.reshape(blocks * PAD // 8, 8, FOURTH), axis=0)
        down_part = dot(act_t[rows, :], cot[:, :, :, :, :, at].reshape(2 * TOK, FOURTH), (1, 0))
        for kind, part in enumerate((up_part, down_part)):
            for b in range(blocks):
                grads[kind, slot + b, :, at] = part[b * PAD : b * PAD + MAIN].astype(BF16)
                end = part[b * PAD + MAIN : b * PAD + MAIN + 16]
                if fourth < 3:
                    grad_tails[kind, slot + b, :, at] = end.astype(BF16)
                    continue
                for other in range(3):
                    to = fourth_of(other)
                    mixed = pack(grad_tails[kind, slot + b, :, to].astype(F32), end, other)
                    grad_tails[kind, slot + b, :, to] = mixed.astype(BF16)

    def send_grads(part, kind, slot, to, device):
        if part == 2:
            return send(grad_tails.at[kind, slot], mail_tails.at[kind, to], device)
        at = pl.ds(part * HALF, HALF)
        return send(grads.at[kind, slot, :, at], mail.at[kind, to, :, at], device)

    gain_acc[...] = jnp.zeros_like(gain_acc)
    forward(0, 1, (0,))

    onward = []
    for ref, copy in ((cot, cot_across), (norm, norm_across)):
        copy.wait_recv()
        src = piece(ref, 1, quarter)
        onward.append([send(src, src, device) for device in (beside, y_at(1), y_at(3))] + [send(src, src, sibling)])
    wait_recv(up_right)
    up_relay = send_block(0, 2, 3, z_at(1))
    wait_recv(down_left)
    down_relay = send_block(1, 1, 3, z_at(3))
    shared = []
    for ref, copies in ((cot, onward[0]), (norm, onward[1])):
        for shift, copy in ((2, copies[0]), (3, copies[1]), (1, copies[2])):
            copy.wait_recv()
            src = piece(ref, 1, (quarter + shift) % 4)
            shared.append(send(src, src, sibling))
    for copy in [onward[0][3], onward[1][3]] + shared:
        copy.wait_recv()

    forward(0, 1, (1,))
    wait_recv(down_right)
    wait_recv(up_left)
    for kind in range(2):
        unpack_block(kind, 1)
        unpack_block(kind, 2)
    forward(1, 2, (0, 1))

    direct = []
    for fourth in range(4):
        backward(0, 3, fourth)
        for part in ((), (0,), (), (1, 2))[fourth]:
            direct.append((send_grads(part, 1, 1, 0, z_at(1)), send_grads(part, 0, 2, 0, z_at(3))))

    wait_recv(up_relay)
    wait_recv(down_relay)
    for kind in range(2):
        unpack_block(kind, 3)
    forward(3, 1, (0, 1))

    for copy in [cot_across, norm_across] + onward[0] + onward[1] + shared:
        copy.wait_send()

    def project(fourth):
        def tile(step, _):
            at = columns(step, STEP, fourth * FOURTH)
            right = weights[1, :, :, at].reshape(4 * PAD, STEP)
            for m in range(2):
                part = dot(act[m * TOK : (m + 1) * TOK, :], right, (1, 0))
                norm[m, :, :, :, :, at] = part.astype(BF16).reshape(4, 2, 2, 32, STEP)
            return 0

        lax.fori_loop(0, FOURTH // STEP, tile, 0)

    def add_core(fourth):
        cols = fourth_of(fourth)

        def tile(step, _):
            at = (step // 8, (step // 2) % 4, step % 2)
            mine = norm[(*at, core, slice(None), cols)].astype(F32)
            theirs = cot[(*at, 0, slice(None), cols)].astype(F32)
            cot[(*at, 0, slice(None), cols)] = (mine + theirs).astype(BF16)
            return 0

        lax.fori_loop(0, 16, tile, 0)

    def microbatch(cx):
        return (cx // 2 + x_hi) % 2

    def first_leg(fourth):
        cores[fourth].wait_recv()
        add_core(fourth)
        cols, turn = fourth_of(fourth), fourth // 2
        copies = []
        for j in range(1, 4):
            to = (x + j) % 4
            if fourth % 2 == 0:
                copies.append(send(cot.at[microbatch(to), :, to % 2, 0, :, cols], x_first.at[turn, j - 1], x_at(j)))
            else:
                copies.append(send(cot.at[:, (y + j) % 4, :, 0, :, cols], y_first.at[turn, j - 1], y_at(j)))
        legs.append(copies)

    def second_leg(fourth):
        for copy in legs[fourth]:
            copy.wait()
        cols, turn = fourth_of(fourth), fourth // 2

        def add(step, _):
            if fourth % 2 == 0:
                total = cot[0, step, x_lo, 0, :, cols].astype(F32)
                for j in range(3):
                    total += x_first[turn, j, step].astype(F32)
                x_first[turn, 0, step] = total.astype(BF16)
            else:
                at = (step // 2, step % 2)
                total = cot[(at[0], y, at[1], 0, slice(None), cols)].astype(F32)
                for j in range(3):
                    total += y_first[(turn, j, *at)].astype(F32)
                y_first[(turn, 0, *at)] = total.astype(BF16)
            return 0

        lax.fori_loop(0, 4, add, 0)
        copies = []
        for j in range(1, 4):
            to = (x + j) % 4
            if fourth % 2 == 0:
                copies.append(send(x_first.at[turn, 0, (y + j) % 4], y_second.at[turn, j - 1], y_at(j)))
            else:
                copies.append(send(y_first.at[turn, 0, microbatch(to), to % 2], x_second.at[turn, j - 1], x_at(j)))
        legs[fourth] = copies

    def last_sum(fourth):
        for copy in legs[fourth]:
            copy.wait()
        cols, turn = fourth_of(fourth), fourth // 2
        if fourth % 2 == 0:
            total, others = x_first[turn, 0, y], y_second
        else:
            total, others = y_first[turn, 0, 0, x_lo], x_second
        total = own_rows[:, cols].astype(F32) + total.astype(F32)
        for j in range(3):
            total += others[turn, j].astype(F32)
        out_ref[:, cols] = total.astype(BF16)

    far, cores, legs = [], [], []
    for fourth in range(4):
        backward(3, 1, fourth)
        for part in ((), (0,), (), (1, 2))[fourth]:
            far.append((send_grads(part, 0, 3, 1, z_at(1)), send_grads(part, 1, 3, 1, z_at(3))))
        pl.semaphore_signal(free_sem, inc=1, device_id=sibling, device_id_type=MESH)
        project(fourth)
        pl.semaphore_wait(free_sem, 1)
        cols = fourth_of(fourth)
        cores.append(send(norm.at[:, :, :, 1 - core, :, cols], cot.at[:, :, :, 0, :, cols], sibling))
        if fourth > 0:
            first_leg(fourth - 1)
    gain_own[...] = jnp.sum(gain_acc[...], axis=0, keepdims=True)
    gain_core = send(gain_own, gain_slots.at[0, 0], sibling)
    first_leg(3)

    def spread(stage, place, others):
        gain_slots[stage, place] = gain_own[...]
        return [send(gain_own, gain_slots.at[stage, place], other) for other in others]

    def gather(stage, copies):
        for copy in copies:
            copy.wait()
        gain_own[...] = (gain_slots[stage, 0] + gain_slots[stage, 1]) + (gain_slots[stage, 2] + gain_slots[stage, 3])

    gain_core.wait()
    gain_own[...] = gain_own[...] + gain_slots[0, 0]
    gain_x = spread(1, x, [x_at(j) for j in range(1, 4)])

    last_leg = []

    def combine(part):
        for copy in far[part]:
            copy.wait_recv()
        pairs = ((0, 1), (1, 2))
        if part == 2:
            for kind, slot in pairs:
                total = grad_tails[kind, slot].astype(F32) + mail_tails[kind, 1].astype(F32)
                grad_tails[kind, slot] = total.astype(BF16)
        else:

            def tile(step, _):
                cols = columns(step, 512, part * HALF)
                for kind, slot in pairs:
                    total = grads[kind, slot, :, cols].astype(F32) + mail[kind, 1, :, cols].astype(F32)
                    grads[kind, slot, :, cols] = total.astype(BF16)
                return 0

            lax.fori_loop(0, HALF // 512, tile, 0)
        last_leg.append((send_grads(part, 0, 1, 2, z_at(1)), send_grads(part, 1, 2, 2, z_at(3))))

    gather(1, gain_x)
    gain_y = spread(2, y, [y_at(j) for j in range(1, 4)])
    second_leg(0)
    second_leg(1)
    combine(0)
    gather(2, gain_y)
    gain_z = spread(3, z, [z_at(j) for j in range(1, 4)])
    second_leg(2)
    second_leg(3)
    combine(1)
    combine(2)

    gather(3, gain_z)
    gain_out_ref[...] = gain_own[...] / gain
    load_own.wait()
    for fourth in range(4):
        last_sum(fourth)

    outputs = (grad_up_ref, grad_down_ref)
    for part in range(3):
        for copy in (*direct[part], *last_leg[part]):
            copy.wait_recv()
        if part == 2:
            for kind, ref in enumerate(outputs):
                fourths = []
                for at in range(3):
                    cols = fourth_of(at)
                    total = grad_tails[kind, 0, :, cols].astype(F32)
                    total += mail_tails[kind, 0, :, cols].astype(F32)
                    total += mail_tails[kind, 2, :, cols].astype(F32)
                    fourths.append(total)
                for at, rows in enumerate(unpack(fourths)):
                    ref[MAIN:OWN, fourth_of(at)] = rows[0 : OWN - MAIN].astype(BF16)
            continue

        def finish(step, _):
            cols = columns(step, 512, part * HALF)
            for kind, ref in enumerate(outputs):
                total = grads[kind, 0, :, cols].astype(F32)
                total += mail[kind, 0, :, cols].astype(F32)
                total += mail[kind, 2, :, cols].astype(F32)
                ref[0:MAIN, cols] = total.astype(BF16)
            return 0

        lax.fori_loop(0, HALF // 512, finish, 0)

    for copies in (up_right, down_left, down_right, up_left, up_relay, down_relay, cores, *direct, *far, *last_leg):
        for copy in copies:
            copy.wait_send()


def copy_kernel(*refs):
    for src, dst in zip(refs[:4], refs[4:]):
        dst[...] = src[...]


COPIES = 96


def body(tokens, cotangent, gain, up_weight, down_weight):
    vmem, anywhere = pl.BlockSpec(memory_space=pltpu.VMEM), pl.BlockSpec(memory_space=pl.ANY)
    rows = (1, 4, 2, 2, 32, D)
    results = (
        jax.ShapeDtypeStruct((32, D), BF16),
        jax.ShapeDtypeStruct((1, D), F32),
        jax.ShapeDtypeStruct((OWN, D), BF16),
        jax.ShapeDtypeStruct((OWN, D), BF16),
    )
    parts = pl.pallas_call(
        kernel,
        out_shape=results,
        in_specs=[anywhere, anywhere, vmem, vmem, vmem],
        out_specs=(vmem, vmem, vmem, vmem),
        scratch_shapes=[
            pltpu.VMEM((2, 4, 2, 2, 32, D), BF16),
            pltpu.VMEM((2, 4, 2, 2, 32, D), BF16),
            pltpu.VMEM((2, 4, PAD, D), BF16),
            pltpu.VMEM((2, 4, 16, TAIL), BF16),
            pltpu.VMEM((2 * TOK, 4 * PAD), BF16),
            pltpu.VMEM((4 * PAD, 2 * TOK), BF16),
            pltpu.VMEM((4 * PAD, 2 * TOK), BF16),
            pltpu.VMEM((2, 2 * TOK, 2 * PAD), F32),
            pltpu.VMEM((2, 4, MAIN, D), BF16),
            pltpu.VMEM((2, 4, 16, TAIL), BF16),
            pltpu.VMEM((2, 3, MAIN, D), BF16),
            pltpu.VMEM((2, 3, 16, TAIL), BF16),
            pltpu.VMEM((2, 3, 4, 32, FOURTH), BF16),
            pltpu.VMEM((2, 3, 2, 2, 32, FOURTH), BF16),
            pltpu.VMEM((2, 3, 32, FOURTH), BF16),
            pltpu.VMEM((2, 3, 32, FOURTH), BF16),
            pltpu.VMEM((32, D), BF16),
            pltpu.VMEM((8, D), F32),
            pltpu.VMEM((1, D), F32),
            pltpu.VMEM((4, 4, 1, D), F32),
            pltpu.SemaphoreType.DMA((COPIES,)),
            pltpu.SemaphoreType.DMA((COPIES,)),
            pltpu.SemaphoreType.DMA((3,)),
            pltpu.SemaphoreType.REGULAR,
        ],
        compiler_params=pltpu.CompilerParams(collective_id=0, has_side_effects=True, vmem_limit_bytes=63 * 2**20),
    )(tokens.reshape(rows), cotangent.reshape(rows), gain[None], up_weight, down_weight)
    out, gain_out, grad_up, grad_down = pl.pallas_call(
        copy_kernel,
        out_shape=results,
        in_specs=[vmem] * 4,
        out_specs=(vmem,) * 4,
    )(*parts)
    return (out[None], gain_out[0], grad_up, grad_down)


def solution(mesh):
    placed = (
        P("blk", None, None),
        P("blk", None, None),
        P(),
        P(("dp", "blk"), None),
        P(("dp", "blk"), None),
    )
    return jax.shard_map(
        body,
        mesh=mesh,
        in_specs=placed,
        out_specs=(P("blk", "dp", None), P(), P(("dp", "blk"), None), P(("dp", "blk"), None)),
        check_vma=False,
    )
```

```python
import jax
import jax.numpy as jnp
from jax import lax
from jax.experimental import pallas as pl
from jax.experimental.pallas import tpu as pltpu
from jax.sharding import PartitionSpec as P

D = 5120
TOK = 512
OWN = 108
MAIN = 96
PAD = 128
STEP = 256
HALF = D // 2
FOURTH = D // 4
TAIL = 3 * FOURTH
MESH = pl.DeviceIdType.MESH
BF16 = jnp.bfloat16
F32 = jnp.float32


def columns(step, size=STEP, first=0):
    return pl.ds(pl.multiple_of(first + step * size, size), size)


def row_numbers(like):
    return lax.broadcasted_iota(jnp.int32, like.shape, 0)


def pack(fourth, last, at):
    return jnp.where(row_numbers(fourth) < 12, fourth, pltpu.roll(last, 12 - 4 * at, 0))


def unpack(fourths):
    row = row_numbers(fourths[0])
    moved = [pltpu.roll(fourth, 4 * at + 4, 0) for at, fourth in enumerate(fourths)]
    last = jnp.where(row < 4, moved[0], jnp.where(row < 8, moved[1], jnp.where(row < 12, moved[2], 0.0)))
    return [jnp.where(row < 12, fourth, 0.0) for fourth in fourths] + [last]


def dot(a, b, over):
    return lax.dot_general(a, b, ((over[:1], over[1:]), ((), ())), preferred_element_type=F32)


def kernel(
    tokens_ref, cotangent_ref, gain_ref, up_ref, down_ref,
    out_ref, gain_out_ref, grad_up_ref, grad_down_ref,
    own, norm, cot, weights, tails, act, act_t, hidden_t, acc, grads, grad_tails, mail, mail_tails,
    x_first, y_first, y_second, x_second,
    own_rows, gain_acc, gain_own, gain_other, gain_half, gain_halves, gain_slots, send_sem, recv_sem, local_sem, free_sem,
):
    dp, blk = lax.axis_index("dp"), lax.axis_index("blk")
    y, x_lo, core = dp // 4, (dp // 2) % 2, dp % 2
    z, x_hi = blk // 2, blk % 2
    x = 2 * x_hi + x_lo

    def chip(cx, cy, cz, cc):
        return (cy * 4 + (cx % 2) * 2 + cc, cz * 2 + cx // 2)

    def x_at(j):
        return chip((x + j) % 4, y, z, core)

    def y_at(j):
        return chip(x, (y + j) % 4, z, core)

    def z_at(j):
        return chip(x, y, (z + j) % 4, core)

    sibling = chip(x, y, z, 1 - core)
    across = chip(3 - x, y, z, core)
    beside = chip(x + 1 - 2 * x_lo, y, z, core)

    count = [0]

    def send(src, dst, device):
        at = count[0]
        count[0] += 1
        copy = pltpu.make_async_remote_copy(
            src_ref=src, dst_ref=dst, send_sem=send_sem.at[at], recv_sem=recv_sem.at[at], device_id=device, device_id_type=MESH
        )
        copy.start()
        return copy

    loads = [pltpu.make_async_copy(ref, own.at[kind], local_sem.at[3 + kind]) for kind, ref in enumerate((up_ref, down_ref))]
    for load in loads:
        load.start()
    load_tokens = pltpu.make_async_copy(tokens_ref.at[0], norm.at[0], local_sem.at[0])
    load_cot = pltpu.make_async_copy(cotangent_ref.at[0], cot.at[0], local_sem.at[1])
    load_own = pltpu.make_async_copy(tokens_ref.at[0, y, x_lo, core], own_rows, local_sem.at[2])
    load_tokens.start()
    load_cot.start()
    load_own.start()

    partners = [x_at(1), x_at(2), x_at(3), y_at(1), y_at(2), y_at(3), z_at(1), z_at(2), z_at(3), sibling]
    barrier = pltpu.get_barrier_semaphore()
    for partner in partners:
        pl.semaphore_signal(barrier, inc=1, device_id=partner, device_id_type=MESH)

    def fourth_of(at):
        return pl.ds(at * FOURTH, FOURTH)

    pl.semaphore_wait(barrier, len(partners))
    for load in loads:
        load.wait()

    def send_main(kind, to, device):
        return send(own.at[kind, pl.ds(0, MAIN)], weights.at[kind, to, pl.ds(0, MAIN)], device)

    def send_tail(kind, to, device):
        return send(tails.at[kind, 0], tails.at[kind, to], device)

    up_right, down_left = [send_main(0, 2, z_at(1))], [send_main(1, 1, z_at(3))]
    down_right, up_left = [send_main(1, 2, z_at(1))], [send_main(0, 1, z_at(3))]

    for kind in range(2):
        weights[kind, 0, MAIN:PAD, :] = jnp.zeros((PAD - MAIN, D), BF16)
        weights[kind, 0, MAIN:OWN, :] = own[kind, MAIN:OWN, :]
        last = weights[kind, 0, MAIN : MAIN + 16, fourth_of(3)].astype(F32)
        for at in range(3):
            rows = weights[kind, 0, MAIN : MAIN + 16, fourth_of(at)].astype(F32)
            tails[kind, 0, :, fourth_of(at)] = pack(rows, last, at).astype(BF16)
    up_right.append(send_tail(0, 2, z_at(1)))
    down_left.append(send_tail(1, 1, z_at(3)))
    down_right.append(send_tail(1, 2, z_at(1)))
    up_left.append(send_tail(0, 1, z_at(3)))
    for kind in range(2):
        weights[kind, 0, 0:MAIN, :] = own[kind, 0:MAIN, :]
        for slot in range(1, 4):
            weights[kind, slot, MAIN + 16 : PAD, :] = jnp.zeros((PAD - MAIN - 16, D), BF16)

    def send_block(kind, slot, to, device):
        return [
            send(weights.at[kind, slot, pl.ds(0, MAIN)], weights.at[kind, to, pl.ds(0, MAIN)], device),
            send(tails.at[kind, slot], tails.at[kind, to], device),
        ]

    def wait_recv(copies):
        for copy in copies:
            copy.wait_recv()

    def unpack_block(kind, slot):
        fourths = unpack([tails[kind, slot, :, fourth_of(at)].astype(F32) for at in range(3)])
        for at in range(4):
            weights[kind, slot, MAIN : MAIN + 16, fourth_of(at)] = fourths[at].astype(BF16)

    quarter = (y + 2 * x_lo) % 4
    quarter_across = (y + 2 - 2 * x_lo) % 4

    def piece(ref, which, q):
        return ref.at[which, q, :, core]

    load_cot.wait()
    cot_across = send(piece(cot, 0, quarter_across), piece(cot, 1, quarter_across), across)

    load_tokens.wait()
    gain = gain_ref[...]

    def normalize(step, _):
        at = (0, step // 8, (step // 4) % 2, (step // 2) % 2, pl.ds(pl.multiple_of((step % 2) * 16, 16), 16))
        rows = norm[at].astype(F32)
        inverse = lax.rsqrt(jnp.mean(rows * rows, axis=-1, keepdims=True) + 1e-05)
        norm[at] = (rows * inverse * gain).astype(BF16)
        return 0

    lax.fori_loop(0, 32, normalize, 0)
    norm_across = send(piece(norm, 0, quarter_across), piece(norm, 1, quarter_across), across)

    def forward(slot, blocks, micros):
        width = blocks * PAD
        tall = len(micros) * TOK
        first_row = micros[0] * TOK
        which = slice(micros[0], micros[0] + len(micros))

        for kind, rows in enumerate((norm, cot)):
            left = rows[which].reshape(tall, D)
            right = weights[kind, slot : slot + blocks].reshape(width, D)
            acc[kind, 0:tall, 0:width] = dot(left, right, (1, 1))

        def finish(step, _):
            rows = columns(step, 128)
            hidden, back = acc[0, rows, 0:width], acc[1, rows, 0:width]
            sig = 1.0 / (1.0 + jnp.exp(-hidden))
            active = hidden * sig
            hidden_grad = back * sig * (1.0 + hidden * (1.0 - sig))
            to = columns(step, 128, first_row)
            act[to, slot * PAD : slot * PAD + width] = active.astype(BF16)
            act_t[slot * PAD : slot * PAD + width, to] = active.T.astype(BF16)
            hidden_t[slot * PAD : slot * PAD + width, to] = hidden_grad.T.astype(BF16)
            return 0

        lax.fori_loop(0, tall // 128, finish, 0)

    def backward(slot, blocks, fourth):
        rows = pl.ds(slot * PAD, blocks * PAD)

        at = fourth_of(fourth)
        up_part = dot(hidden_t[rows, :], norm[:, :, :, :, :, at].reshape(2 * TOK, FOURTH), (1, 0))
        terms = weights[0, slot : slot + blocks, :, at].reshape(blocks * PAD, FOURTH).astype(F32) * up_part
        gain_acc[:, at] += jnp.sum(terms.reshape(blocks * PAD // 8, 8, FOURTH), axis=0)
        down_part = dot(act_t[rows, :], cot[:, :, :, :, :, at].reshape(2 * TOK, FOURTH), (1, 0))
        for kind, part in enumerate((up_part, down_part)):
            for b in range(blocks):
                grads[kind, slot + b, :, at] = part[b * PAD : b * PAD + MAIN].astype(BF16)
                end = part[b * PAD + MAIN : b * PAD + MAIN + 16]
                if fourth < 3:
                    grad_tails[kind, slot + b, :, at] = end.astype(BF16)
                    continue
                for other in range(3):
                    to = fourth_of(other)
                    mixed = pack(grad_tails[kind, slot + b, :, to].astype(F32), end, other)
                    grad_tails[kind, slot + b, :, to] = mixed.astype(BF16)

    def send_grads(part, kind, slot, to, device):
        if part == 2:
            return send(grad_tails.at[kind, slot], mail_tails.at[kind, to], device)
        at = pl.ds(part * HALF, HALF)
        return send(grads.at[kind, slot, :, at], mail.at[kind, to, :, at], device)

    gain_acc[...] = jnp.zeros_like(gain_acc)
    forward(0, 1, (0,))

    onward = []
    for ref, copy in ((cot, cot_across), (norm, norm_across)):
        copy.wait_recv()
        src = piece(ref, 1, quarter)
        onward.append([send(src, src, device) for device in (beside, y_at(1), y_at(3))] + [send(src, src, sibling)])
    wait_recv(up_right)
    up_relay = send_block(0, 2, 3, z_at(1))
    wait_recv(down_left)
    down_relay = send_block(1, 1, 3, z_at(3))
    shared = []
    for ref, copies in ((cot, onward[0]), (norm, onward[1])):
        for shift, copy in ((2, copies[0]), (3, copies[1]), (1, copies[2])):
            copy.wait_recv()
            src = piece(ref, 1, (quarter + shift) % 4)
            shared.append(send(src, src, sibling))
    for copy in [onward[0][3], onward[1][3]] + shared:
        copy.wait_recv()

    forward(0, 1, (1,))
    wait_recv(down_right)
    wait_recv(up_left)
    for kind in range(2):
        unpack_block(kind, 1)
        unpack_block(kind, 2)
    forward(1, 2, (0, 1))

    direct = []

    def send_direct(part):
        direct.append((send_grads(part, 1, 1, 0, z_at(1)), send_grads(part, 0, 2, 0, z_at(3))))

    for fourth in range(4):
        backward(0, 3, fourth)
        for part in ((), (0,), (), (1, 2))[fourth]:
            send_direct(part)

    wait_recv(up_relay)
    wait_recv(down_relay)
    for kind in range(2):
        unpack_block(kind, 3)
    forward(3, 1, (0, 1))

    for copy in [cot_across, norm_across] + onward[0] + onward[1] + shared:
        copy.wait_send()

    def project(fourth):
        def tile(step, _):
            at = columns(step, STEP, fourth * FOURTH)
            right = weights[1, :, :, at].reshape(4 * PAD, STEP)
            for m in range(2):
                part = dot(act[m * TOK : (m + 1) * TOK, :], right, (1, 0))
                norm[m, :, :, :, :, at] = part.astype(BF16).reshape(4, 2, 2, 32, STEP)
            return 0

        lax.fori_loop(0, FOURTH // STEP, tile, 0)

    def add_core(fourth):
        cols = fourth_of(fourth)

        def tile(step, _):
            at = (step // 8, (step // 2) % 4, step % 2)
            mine = norm[(*at, core, slice(None), cols)].astype(F32)
            theirs = cot[(*at, 0, slice(None), cols)].astype(F32)
            cot[(*at, 0, slice(None), cols)] = (mine + theirs).astype(BF16)
            return 0

        lax.fori_loop(0, 16, tile, 0)

    def microbatch(cx):
        return (cx // 2 + x_hi) % 2

    def first_leg(fourth):
        cores[fourth].wait_recv()
        add_core(fourth)
        cols, turn = fourth_of(fourth), fourth // 2
        copies = []
        for j in range(1, 4):
            to = (x + j) % 4
            if fourth % 2 == 0:
                copies.append(send(cot.at[microbatch(to), :, to % 2, 0, :, cols], x_first.at[turn, j - 1], x_at(j)))
            else:
                copies.append(send(cot.at[:, (y + j) % 4, :, 0, :, cols], y_first.at[turn, j - 1], y_at(j)))
        legs.append(copies)

    def second_leg(fourth):
        for copy in legs[fourth]:
            copy.wait()
        cols, turn = fourth_of(fourth), fourth // 2

        def add(step, _):
            if fourth % 2 == 0:
                total = cot[0, step, x_lo, 0, :, cols].astype(F32)
                for j in range(3):
                    total += x_first[turn, j, step].astype(F32)
                x_first[turn, 0, step] = total.astype(BF16)
            else:
                at = (step // 2, step % 2)
                total = cot[(at[0], y, at[1], 0, slice(None), cols)].astype(F32)
                for j in range(3):
                    total += y_first[(turn, j, *at)].astype(F32)
                y_first[(turn, 0, *at)] = total.astype(BF16)
            return 0

        lax.fori_loop(0, 4, add, 0)
        copies = []
        for j in range(1, 4):
            to = (x + j) % 4
            if fourth % 2 == 0:
                copies.append(send(x_first.at[turn, 0, (y + j) % 4], y_second.at[turn, j - 1], y_at(j)))
            else:
                copies.append(send(y_first.at[turn, 0, microbatch(to), to % 2], x_second.at[turn, j - 1], x_at(j)))
        legs[fourth] = copies

    def last_sum(fourth):
        for copy in legs[fourth]:
            copy.wait()
        cols, turn = fourth_of(fourth), fourth // 2
        if fourth % 2 == 0:
            total, others = x_first[turn, 0, y], y_second
        else:
            total, others = y_first[turn, 0, 0, x_lo], x_second
        total = own_rows[:, cols].astype(F32) + total.astype(F32)
        for j in range(3):
            total += others[turn, j].astype(F32)
        out_ref[:, cols] = total.astype(BF16)

    far, cores, legs = [], [], []

    def send_far(part):
        far.append((send_grads(part, 0, 3, 1, z_at(1)), send_grads(part, 1, 3, 1, z_at(3))))

    def share(fourth):
        project(fourth)
        pl.semaphore_wait(free_sem, 1)
        cols = fourth_of(fourth)
        cores.append(send(norm.at[:, :, :, 1 - core, :, cols], cot.at[:, :, :, 0, :, cols], sibling))

    for fourth in range(4):
        backward(3, 1, fourth)
        pl.semaphore_signal(free_sem, inc=1, device_id=sibling, device_id_type=MESH)
        if fourth == 1:
            send_far(0)
            share(0)
        if fourth == 3:
            send_far(1)
            send_far(2)
    for fourth in range(1, 4):
        share(fourth)
        first_leg(fourth - 1)
    gain_own[...] = jnp.sum(gain_acc[...], axis=0, keepdims=True)
    gain_core = send(gain_own, gain_other, sibling)
    first_leg(3)

    def spread(stage, place, others):
        gain_slots[stage, place] = gain_half[...]
        return [send(gain_half, gain_slots.at[stage, place], other) for other in others]

    def gather(stage, copies):
        for copy in copies:
            copy.wait()
        gain_half[...] = (gain_slots[stage, 0] + gain_slots[stage, 1]) + (gain_slots[stage, 2] + gain_slots[stage, 3])

    gain_core.wait()
    own_half = pl.ds(pl.multiple_of(core * HALF, HALF), HALF)
    gain_half[...] = gain_own[:, own_half] + gain_other[:, own_half]
    gain_z = spread(0, z, [z_at(j) for j in range(1, 4)])

    last_leg = []

    def combine(part):
        for copy in far[part]:
            copy.wait_recv()
        pairs = ((0, 1), (1, 2))
        if part == 2:
            for kind, slot in pairs:
                total = grad_tails[kind, slot].astype(F32) + mail_tails[kind, 1].astype(F32)
                grad_tails[kind, slot] = total.astype(BF16)
        else:

            def tile(step, _):
                cols = columns(step, 512, part * HALF)
                for kind, slot in pairs:
                    total = grads[kind, slot, :, cols].astype(F32) + mail[kind, 1, :, cols].astype(F32)
                    grads[kind, slot, :, cols] = total.astype(BF16)
                return 0

            lax.fori_loop(0, HALF // 512, tile, 0)
        last_leg.append((send_grads(part, 0, 1, 2, z_at(1)), send_grads(part, 1, 2, 2, z_at(3))))

    second_leg(0)
    second_leg(1)
    combine(0)
    second_leg(2)
    combine(1)
    combine(2)
    second_leg(3)

    load_own.wait()
    gather(0, gain_z)
    gain_x = spread(1, x, [x_at(j) for j in range(1, 4)])
    last_sum(0)
    last_sum(1)
    gather(1, gain_x)
    gain_y = spread(2, y, [y_at(j) for j in range(1, 4)])
    last_sum(2)
    last_sum(3)
    gather(2, gain_y)
    gain_last = send(gain_half, gain_halves.at[core], sibling)
    gain_halves[core] = gain_half[...]

    outputs = (grad_up_ref, grad_down_ref)
    for part in range(3):
        for copy in (*direct[part], *last_leg[part]):
            copy.wait_recv()
        if part == 2:
            gain_last.wait()
            for at in range(2):
                cols = pl.ds(at * HALF, HALF)
                gain_out_ref[:, cols] = gain_halves[at] / gain_ref[:, cols]
            for kind, ref in enumerate(outputs):
                fourths = []
                for at in range(3):
                    cols = fourth_of(at)
                    total = grad_tails[kind, 0, :, cols].astype(F32)
                    total += mail_tails[kind, 0, :, cols].astype(F32)
                    total += mail_tails[kind, 2, :, cols].astype(F32)
                    fourths.append(total)
                for at, rows in enumerate(unpack(fourths)):
                    ref[MAIN:OWN, fourth_of(at)] = rows[0 : OWN - MAIN].astype(BF16)
            continue

        def finish(step, _):
            cols = columns(step, 512, part * HALF)
            for kind, ref in enumerate(outputs):
                total = grads[kind, 0, :, cols].astype(F32)
                total += mail[kind, 0, :, cols].astype(F32)
                total += mail[kind, 2, :, cols].astype(F32)
                ref[0:MAIN, cols] = total.astype(BF16)
            return 0

        lax.fori_loop(0, HALF // 512, finish, 0)

    for copies in (up_right, down_left, down_right, up_left, up_relay, down_relay, cores, *direct, *far, *last_leg):
        for copy in copies:
            copy.wait_send()


def copy_kernel(*refs):
    sources, targets, held, sems = refs[:4], refs[4:8], refs[8:12], refs[12]
    loads = [pltpu.make_async_copy(sources[i], held[i], sems.at[0, i]) for i in range(4)]
    stores = [pltpu.make_async_copy(held[i], targets[i], sems.at[1, i]) for i in range(4)]
    for load in loads:
        load.start()
    for load, store in zip(loads, stores):
        load.wait()
        store.start()
    for store in stores:
        store.wait()


COPIES = 96


def body(tokens, cotangent, gain, up_weight, down_weight):
    vmem, anywhere = pl.BlockSpec(memory_space=pltpu.VMEM), pl.BlockSpec(memory_space=pl.ANY)
    rows = (1, 4, 2, 2, 32, D)
    results = (
        jax.ShapeDtypeStruct((32, D), BF16),
        jax.ShapeDtypeStruct((1, D), F32),
        jax.ShapeDtypeStruct((OWN, D), BF16),
        jax.ShapeDtypeStruct((OWN, D), BF16),
    )
    parts = pl.pallas_call(
        kernel,
        out_shape=results,
        in_specs=[anywhere, anywhere, vmem, anywhere, anywhere],
        out_specs=(vmem, vmem, vmem, vmem),
        scratch_shapes=[
            pltpu.VMEM((2, OWN, D), BF16),
            pltpu.VMEM((2, 4, 2, 2, 32, D), BF16),
            pltpu.VMEM((2, 4, 2, 2, 32, D), BF16),
            pltpu.VMEM((2, 4, PAD, D), BF16),
            pltpu.VMEM((2, 4, 16, TAIL), BF16),
            pltpu.VMEM((2 * TOK, 4 * PAD), BF16),
            pltpu.VMEM((4 * PAD, 2 * TOK), BF16),
            pltpu.VMEM((4 * PAD, 2 * TOK), BF16),
            pltpu.VMEM((2, 2 * TOK, 2 * PAD), F32),
            pltpu.VMEM((2, 4, MAIN, D), BF16),
            pltpu.VMEM((2, 4, 16, TAIL), BF16),
            pltpu.VMEM((2, 3, MAIN, D), BF16),
            pltpu.VMEM((2, 3, 16, TAIL), BF16),
            pltpu.VMEM((2, 3, 4, 32, FOURTH), BF16),
            pltpu.VMEM((2, 3, 2, 2, 32, FOURTH), BF16),
            pltpu.VMEM((2, 3, 32, FOURTH), BF16),
            pltpu.VMEM((2, 3, 32, FOURTH), BF16),
            pltpu.VMEM((32, D), BF16),
            pltpu.VMEM((8, D), F32),
            pltpu.VMEM((1, D), F32),
            pltpu.VMEM((1, D), F32),
            pltpu.VMEM((1, HALF), F32),
            pltpu.VMEM((2, 1, HALF), F32),
            pltpu.VMEM((3, 4, 1, HALF), F32),
            pltpu.SemaphoreType.DMA((COPIES,)),
            pltpu.SemaphoreType.DMA((COPIES,)),
            pltpu.SemaphoreType.DMA((5,)),
            pltpu.SemaphoreType.REGULAR,
        ],
        compiler_params=pltpu.CompilerParams(collective_id=0, has_side_effects=True, vmem_limit_bytes=63 * 2**20),
    )(tokens.reshape(rows), cotangent.reshape(rows), gain[None], up_weight, down_weight)
    out, gain_out, grad_up, grad_down = pl.pallas_call(
        copy_kernel,
        out_shape=results,
        in_specs=[anywhere] * 4,
        out_specs=(anywhere,) * 4,
        scratch_shapes=[pltpu.VMEM(part.shape, part.dtype) for part in results] + [pltpu.SemaphoreType.DMA((2, 4))],
    )(*parts)
    return (out[None], gain_out[0], grad_up, grad_down)


def solution(mesh):
    placed = (
        P("blk", None, None),
        P("blk", None, None),
        P(),
        P(("dp", "blk"), None),
        P(("dp", "blk"), None),
    )
    return jax.shard_map(
        body,
        mesh=mesh,
        in_specs=placed,
        out_specs=(P("blk", "dp", None), P(), P(("dp", "blk"), None), P(("dp", "blk"), None)),
        check_vma=False,
    )
```

```python
import jax
import jax.numpy as jnp
from jax import lax
from jax.experimental import pallas as pl
from jax.experimental.pallas import tpu as pltpu
from jax.sharding import PartitionSpec as P

D = 5120
TOK = 512
OWN = 108
MAIN = 96
PAD = 128
STEP = 256
HALF = D // 2
FOURTH = D // 4
TAIL = 3 * FOURTH
MESH = pl.DeviceIdType.MESH
BF16 = jnp.bfloat16
F32 = jnp.float32


def columns(step, size=STEP, first=0):
    return pl.ds(pl.multiple_of(first + step * size, size), size)


def row_numbers(like):
    return lax.broadcasted_iota(jnp.int32, like.shape, 0)


def pack(fourth, last, at):
    return jnp.where(row_numbers(fourth) < 12, fourth, pltpu.roll(last, 12 - 4 * at, 0))


def unpack(fourths):
    row = row_numbers(fourths[0])
    moved = [pltpu.roll(fourth, 4 * at + 4, 0) for at, fourth in enumerate(fourths)]
    last = jnp.where(row < 4, moved[0], jnp.where(row < 8, moved[1], jnp.where(row < 12, moved[2], 0.0)))
    return [jnp.where(row < 12, fourth, 0.0) for fourth in fourths] + [last]


def dot(a, b, over):
    return lax.dot_general(a, b, ((over[:1], over[1:]), ((), ())), preferred_element_type=F32)


def kernel(
    tokens_ref, cotangent_ref, gain_ref, up_ref, down_ref,
    out_ref, gain_out_ref, sum_ref, sum_tail_ref, last_tail_ref,
    own, norm, cot, weights, tails, act, act_t, hidden_t, acc, grads, grad_tails, mail, mail_tails,
    x_first, y_first, y_second, x_second,
    own_rows, out_rows, gain_acc, gain_own, gain_other, gain_half, gain_halves, gain_slots, send_sem, recv_sem, local_sem, store_sem, free_sem,
):
    dp, blk = lax.axis_index("dp"), lax.axis_index("blk")
    y, x_lo, core = dp // 4, (dp // 2) % 2, dp % 2
    z, x_hi = blk // 2, blk % 2
    x = 2 * x_hi + x_lo

    def chip(cx, cy, cz, cc):
        return (cy * 4 + (cx % 2) * 2 + cc, cz * 2 + cx // 2)

    def x_at(j):
        return chip((x + j) % 4, y, z, core)

    def y_at(j):
        return chip(x, (y + j) % 4, z, core)

    def z_at(j):
        return chip(x, y, (z + j) % 4, core)

    sibling = chip(x, y, z, 1 - core)
    across = chip(3 - x, y, z, core)
    beside = chip(x + 1 - 2 * x_lo, y, z, core)

    count = [0]

    def send(src, dst, device):
        at = count[0]
        count[0] += 1
        copy = pltpu.make_async_remote_copy(
            src_ref=src, dst_ref=dst, send_sem=send_sem.at[at], recv_sem=recv_sem.at[at], device_id=device, device_id_type=MESH
        )
        copy.start()
        return copy

    loads = [pltpu.make_async_copy(ref, own.at[kind], local_sem.at[3 + kind]) for kind, ref in enumerate((up_ref, down_ref))]
    for load in loads:
        load.start()
    load_tokens = pltpu.make_async_copy(tokens_ref.at[0], norm.at[0], local_sem.at[0])
    load_cot = pltpu.make_async_copy(cotangent_ref.at[0], cot.at[0], local_sem.at[1])
    load_own = pltpu.make_async_copy(tokens_ref.at[0, y, x_lo, core], own_rows, local_sem.at[2])
    load_tokens.start()
    load_cot.start()
    load_own.start()

    partners = [x_at(1), x_at(2), x_at(3), y_at(1), y_at(2), y_at(3), z_at(1), z_at(2), z_at(3), sibling]
    barrier = pltpu.get_barrier_semaphore()
    for partner in partners:
        pl.semaphore_signal(barrier, inc=1, device_id=partner, device_id_type=MESH)

    def fourth_of(at):
        return pl.ds(at * FOURTH, FOURTH)

    pl.semaphore_wait(barrier, len(partners))

    def send_main(kind, to, device):
        return send((up_ref, down_ref)[kind].at[pl.ds(0, MAIN)], weights.at[kind, to, pl.ds(0, MAIN)], device)

    def send_tail(kind, to, device):
        return send(tails.at[kind, 0], tails.at[kind, to], device)

    up_right, down_left = [send_main(0, 2, z_at(1))], [send_main(1, 1, z_at(3))]
    down_right, up_left = [send_main(1, 2, z_at(1))], [send_main(0, 1, z_at(3))]

    for load in loads:
        load.wait()
    for kind in range(2):
        weights[kind, 0, MAIN:PAD, :] = jnp.zeros((PAD - MAIN, D), BF16)
        weights[kind, 0, MAIN:OWN, :] = own[kind, MAIN:OWN, :]
        last = weights[kind, 0, MAIN : MAIN + 16, fourth_of(3)].astype(F32)
        for at in range(3):
            rows = weights[kind, 0, MAIN : MAIN + 16, fourth_of(at)].astype(F32)
            tails[kind, 0, :, fourth_of(at)] = pack(rows, last, at).astype(BF16)
    up_right.append(send_tail(0, 2, z_at(1)))
    down_left.append(send_tail(1, 1, z_at(3)))
    down_right.append(send_tail(1, 2, z_at(1)))
    up_left.append(send_tail(0, 1, z_at(3)))
    for kind in range(2):
        weights[kind, 0, 0:MAIN, :] = own[kind, 0:MAIN, :]
        for slot in range(1, 4):
            weights[kind, slot, MAIN + 16 : PAD, :] = jnp.zeros((PAD - MAIN - 16, D), BF16)

    def send_block(kind, slot, to, device):
        return [
            send(weights.at[kind, slot, pl.ds(0, MAIN)], weights.at[kind, to, pl.ds(0, MAIN)], device),
            send(tails.at[kind, slot], tails.at[kind, to], device),
        ]

    def wait_recv(copies):
        for copy in copies:
            copy.wait_recv()

    def unpack_block(kind, slot):
        fourths = unpack([tails[kind, slot, :, fourth_of(at)].astype(F32) for at in range(3)])
        for at in range(4):
            weights[kind, slot, MAIN : MAIN + 16, fourth_of(at)] = fourths[at].astype(BF16)

    quarter = (y + 2 * x_lo) % 4
    quarter_across = (y + 2 - 2 * x_lo) % 4

    def piece(ref, which, q):
        return ref.at[which, q, :, core]

    load_cot.wait()
    cot_across = send(piece(cot, 0, quarter_across), piece(cot, 1, quarter_across), across)

    load_tokens.wait()
    gain = gain_ref[...]

    def normalize(step, _):
        at = (0, step // 8, (step // 4) % 2, (step // 2) % 2, pl.ds(pl.multiple_of((step % 2) * 16, 16), 16))
        rows = norm[at].astype(F32)
        inverse = lax.rsqrt(jnp.mean(rows * rows, axis=-1, keepdims=True) + 1e-05)
        norm[at] = (rows * inverse * gain).astype(BF16)
        return 0

    lax.fori_loop(0, 32, normalize, 0)
    norm_across = send(piece(norm, 0, quarter_across), piece(norm, 1, quarter_across), across)

    def forward(slot, blocks, micros):
        width = blocks * PAD
        tall = len(micros) * TOK
        first_row = micros[0] * TOK
        which = slice(micros[0], micros[0] + len(micros))

        for kind, rows in enumerate((norm, cot)):
            left = rows[which].reshape(tall, D)
            right = weights[kind, slot : slot + blocks].reshape(width, D)
            acc[kind, 0:tall, 0:width] = dot(left, right, (1, 1))

        def finish(step, _):
            rows = columns(step, 128)
            hidden, back = acc[0, rows, 0:width], acc[1, rows, 0:width]
            sig = 1.0 / (1.0 + jnp.exp(-hidden))
            active = hidden * sig
            hidden_grad = back * sig * (1.0 + hidden * (1.0 - sig))
            to = columns(step, 128, first_row)
            act[to, slot * PAD : slot * PAD + width] = active.astype(BF16)
            act_t[slot * PAD : slot * PAD + width, to] = active.T.astype(BF16)
            hidden_t[slot * PAD : slot * PAD + width, to] = hidden_grad.T.astype(BF16)
            return 0

        lax.fori_loop(0, tall // 128, finish, 0)

    def backward(slot, blocks, fourth):
        rows = pl.ds(slot * PAD, blocks * PAD)

        at = fourth_of(fourth)
        up_part = dot(hidden_t[rows, :], norm[:, :, :, :, :, at].reshape(2 * TOK, FOURTH), (1, 0))
        terms = weights[0, slot : slot + blocks, :, at].reshape(blocks * PAD, FOURTH).astype(F32) * up_part
        gain_acc[:, at] += jnp.sum(terms.reshape(blocks * PAD // 8, 8, FOURTH), axis=0)
        down_part = dot(act_t[rows, :], cot[:, :, :, :, :, at].reshape(2 * TOK, FOURTH), (1, 0))
        for kind, part in enumerate((up_part, down_part)):
            for b in range(blocks):
                grads[kind, slot + b, :, at] = part[b * PAD : b * PAD + MAIN].astype(BF16)
                end = part[b * PAD + MAIN : b * PAD + MAIN + 16]
                if fourth < 3:
                    grad_tails[kind, slot + b, :, at] = end.astype(BF16)
                    continue
                for other in range(3):
                    to = fourth_of(other)
                    mixed = pack(grad_tails[kind, slot + b, :, to].astype(F32), end, other)
                    grad_tails[kind, slot + b, :, to] = mixed.astype(BF16)

    def send_grads(part, kind, slot, to, device):
        if part == 2:
            target = last_tail_ref.at[kind] if to == 2 else mail_tails.at[kind, to]
            return send(grad_tails.at[kind, slot], target, device)
        at = pl.ds(part * HALF, HALF)
        return send(grads.at[kind, slot, :, at], mail.at[kind, to, :, at], device)

    gain_acc[...] = jnp.zeros_like(gain_acc)
    forward(0, 1, (0,))

    onward = []
    for ref, copy in ((cot, cot_across), (norm, norm_across)):
        copy.wait_recv()
        src = piece(ref, 1, quarter)
        onward.append([send(src, src, device) for device in (beside, y_at(1), y_at(3))] + [send(src, src, sibling)])
    wait_recv(up_right)
    up_relay = send_block(0, 2, 3, z_at(1))
    wait_recv(down_left)
    down_relay = send_block(1, 1, 3, z_at(3))
    shared = []
    for ref, copies in ((cot, onward[0]), (norm, onward[1])):
        for shift, copy in ((2, copies[0]), (3, copies[1]), (1, copies[2])):
            copy.wait_recv()
            src = piece(ref, 1, (quarter + shift) % 4)
            shared.append(send(src, src, sibling))
    for copy in [onward[0][3], onward[1][3]] + shared:
        copy.wait_recv()

    forward(0, 1, (1,))
    wait_recv(down_right)
    wait_recv(up_left)
    for kind in range(2):
        unpack_block(kind, 1)
        unpack_block(kind, 2)
    forward(1, 2, (0, 1))

    direct = []

    def send_direct(part):
        direct.append((send_grads(part, 1, 1, 0, z_at(1)), send_grads(part, 0, 2, 0, z_at(3))))

    for fourth in range(4):
        backward(0, 3, fourth)
        for part in ((), (0,), (), (1, 2))[fourth]:
            send_direct(part)

    wait_recv(up_relay)
    wait_recv(down_relay)
    for kind in range(2):
        unpack_block(kind, 3)
    forward(3, 1, (0, 1))

    for copy in [cot_across, norm_across] + onward[0] + onward[1] + shared:
        copy.wait_send()

    def project(fourth):
        def tile(step, _):
            at = columns(step, STEP, fourth * FOURTH)
            right = weights[1, :, :, at].reshape(4 * PAD, STEP)
            for m in range(2):
                part = dot(act[m * TOK : (m + 1) * TOK, :], right, (1, 0))
                norm[m, :, :, :, :, at] = part.astype(BF16).reshape(4, 2, 2, 32, STEP)
            return 0

        lax.fori_loop(0, FOURTH // STEP, tile, 0)

    def add_core(fourth):
        cols = fourth_of(fourth)

        def tile(step, _):
            at = (step // 8, (step // 2) % 4, step % 2)
            mine = norm[(*at, core, slice(None), cols)].astype(F32)
            theirs = cot[(*at, 0, slice(None), cols)].astype(F32)
            cot[(*at, 0, slice(None), cols)] = (mine + theirs).astype(BF16)
            return 0

        lax.fori_loop(0, 16, tile, 0)

    def microbatch(cx):
        return (cx // 2 + x_hi) % 2

    def first_leg(fourth):
        cores[fourth].wait_recv()
        add_core(fourth)
        cols, turn = fourth_of(fourth), fourth // 2
        copies = []
        for j in range(1, 4):
            to = (x + j) % 4
            if fourth % 2 == 0:
                copies.append(send(cot.at[microbatch(to), :, to % 2, 0, :, cols], x_first.at[turn, j - 1], x_at(j)))
            else:
                copies.append(send(cot.at[:, (y + j) % 4, :, 0, :, cols], y_first.at[turn, j - 1], y_at(j)))
        legs.append(copies)

    def second_leg(fourth):
        for copy in legs[fourth]:
            copy.wait()
        cols, turn = fourth_of(fourth), fourth // 2

        def add(step, _):
            if fourth % 2 == 0:
                total = cot[0, step, x_lo, 0, :, cols].astype(F32)
                for j in range(3):
                    total += x_first[turn, j, step].astype(F32)
                x_first[turn, 0, step] = total.astype(BF16)
            else:
                at = (step // 2, step % 2)
                total = cot[(at[0], y, at[1], 0, slice(None), cols)].astype(F32)
                for j in range(3):
                    total += y_first[(turn, j, *at)].astype(F32)
                y_first[(turn, 0, *at)] = total.astype(BF16)
            return 0

        lax.fori_loop(0, 4, add, 0)
        copies = []
        for j in range(1, 4):
            to = (x + j) % 4
            if fourth % 2 == 0:
                copies.append(send(x_first.at[turn, 0, (y + j) % 4], y_second.at[turn, j - 1], y_at(j)))
            else:
                copies.append(send(y_first.at[turn, 0, microbatch(to), to % 2], x_second.at[turn, j - 1], x_at(j)))
        legs[fourth] = copies

    def last_sum(fourth):
        for copy in legs[fourth]:
            copy.wait()
        cols, turn = fourth_of(fourth), fourth // 2
        if fourth % 2 == 0:
            total, others = x_first[turn, 0, y], y_second
        else:
            total, others = y_first[turn, 0, 0, x_lo], x_second
        total = own_rows[:, cols].astype(F32) + total.astype(F32)
        for j in range(3):
            total += others[turn, j].astype(F32)
        out_rows[:, cols] = total.astype(BF16)

    far, cores, legs = [], [], []

    def send_far(part):
        far.append((send_grads(part, 0, 3, 1, z_at(1)), send_grads(part, 1, 3, 1, z_at(3))))

    def share(fourth):
        project(fourth)
        pl.semaphore_wait(free_sem, 1)
        cols = fourth_of(fourth)
        cores.append(send(norm.at[:, :, :, 1 - core, :, cols], cot.at[:, :, :, 0, :, cols], sibling))

    for fourth in range(4):
        backward(3, 1, fourth)
        pl.semaphore_signal(free_sem, inc=1, device_id=sibling, device_id_type=MESH)
        if fourth == 1:
            send_far(0)
            share(0)
        if fourth == 3:
            send_far(1)
            send_far(2)
    for fourth in range(1, 4):
        share(fourth)
        first_leg(fourth - 1)
    gain_own[...] = jnp.sum(gain_acc[...], axis=0, keepdims=True)
    gain_core = send(gain_own, gain_other, sibling)
    first_leg(3)

    def spread(stage, place, others):
        gain_slots[stage, place] = gain_half[...]
        return [send(gain_half, gain_slots.at[stage, place], other) for other in others]

    def gather(stage, copies):
        for copy in copies:
            copy.wait()
        gain_half[...] = (gain_slots[stage, 0] + gain_slots[stage, 1]) + (gain_slots[stage, 2] + gain_slots[stage, 3])

    gain_core.wait()
    own_half = pl.ds(pl.multiple_of(core * HALF, HALF), HALF)
    gain_half[...] = gain_own[:, own_half] + gain_other[:, own_half]
    gain_z = spread(0, z, [z_at(j) for j in range(1, 4)])

    last_leg = []

    def combine(part):
        for copy in far[part]:
            copy.wait_recv()
        pairs = ((0, 1), (1, 2))
        if part == 2:
            for kind, slot in pairs:
                total = grad_tails[kind, slot].astype(F32) + mail_tails[kind, 1].astype(F32)
                grad_tails[kind, slot] = total.astype(BF16)
        else:

            def tile(step, _):
                cols = columns(step, 512, part * HALF)
                for kind, slot in pairs:
                    total = grads[kind, slot, :, cols].astype(F32) + mail[kind, 1, :, cols].astype(F32)
                    grads[kind, slot, :, cols] = total.astype(BF16)
                return 0

            lax.fori_loop(0, HALF // 512, tile, 0)
        last_leg.append((send_grads(part, 0, 1, 2, z_at(1)), send_grads(part, 1, 2, 2, z_at(3))))

    second_leg(0)
    second_leg(1)
    combine(0)
    second_leg(2)
    combine(1)
    combine(2)
    second_leg(3)

    load_own.wait()
    gather(0, gain_z)
    gain_x = spread(1, x, [x_at(j) for j in range(1, 4)])
    last_sum(0)
    last_sum(1)
    gather(1, gain_x)
    gain_y = spread(2, y, [y_at(j) for j in range(1, 4)])
    last_sum(2)
    last_sum(3)
    gather(2, gain_y)
    gain_last = send(gain_half, gain_halves.at[core], sibling)
    gain_halves[core] = gain_half[...]

    stores = [pltpu.make_async_copy(out_rows, out_ref, local_sem.at[0])]
    stores[0].start()

    def store(src, dst):
        stores.append(pltpu.make_async_copy(src, dst, store_sem.at[len(stores) - 1]))
        stores[-1].start()

    for copy in direct[2]:
        copy.wait_recv()
    for kind in range(2):
        total = grad_tails[kind, 0].astype(F32) + mail_tails[kind, 0].astype(F32)
        grad_tails[kind, 0] = total.astype(BF16)
        store(grad_tails.at[kind, 0], sum_tail_ref.at[kind])
    gain_last.wait()
    for at in range(2):
        cols = pl.ds(at * HALF, HALF)
        gain_out_ref[:, cols] = gain_halves[at] / gain_ref[:, cols]
    for part in range(2):
        for copy in (*direct[part], *last_leg[part]):
            copy.wait_recv()

        def finish(step, _):
            cols = columns(step, 512, part * HALF)
            for kind in range(2):
                total = grads[kind, 0, :, cols].astype(F32)
                total += mail[kind, 0, :, cols].astype(F32)
                total += mail[kind, 2, :, cols].astype(F32)
                grads[kind, 0, :, cols] = total.astype(BF16)
            return 0

        lax.fori_loop(0, HALF // 512, finish, 0)
        for kind in range(2):
            at = pl.ds(part * HALF, HALF)
            store(grads.at[kind, 0, :, at], sum_ref.at[kind, :, at])
    for copy in last_leg[2]:
        copy.wait_recv()
    for copy in stores:
        copy.wait()

    for copies in (up_right, down_left, down_right, up_left, up_relay, down_relay, cores, *direct, *far, *last_leg):
        for copy in copies:
            copy.wait_send()


def closing_kernel(
    rows_ref, gain_ref, sum_ref, sum_tail_ref, last_tail_ref, out_ref, gain_out_ref, grad_up_ref, grad_down_ref,
    rows, gain, tails, tail_lasts, result, load_sem, store_sem,
):
    loads = []

    def load(src, dst):
        loads.append(pltpu.make_async_copy(src, dst, load_sem.at[len(loads)]))
        loads[-1].start()
        return loads[-1]

    small = [load(sum_tail_ref, tails), load(last_tail_ref, tail_lasts)]
    pieces = [(kind, pl.ds(part * HALF, HALF)) for kind in range(2) for part in range(2)]
    large = [load(sum_ref.at[kind, :, at], result.at[kind, pl.ds(0, MAIN), at]) for kind, at in pieces]
    copies = [load(rows_ref, rows), load(gain_ref, gain)]
    stores = [
        pltpu.make_async_copy(rows, out_ref, store_sem.at[0]),
        pltpu.make_async_copy(gain, gain_out_ref, store_sem.at[1]),
    ]
    for index, (kind, at) in enumerate(pieces):
        target = (grad_up_ref, grad_down_ref)[kind].at[:, at]
        stores.append(pltpu.make_async_copy(result.at[kind, :, at], target, store_sem.at[2 + index]))
    for copy in small:
        copy.wait()
    for kind in range(2):
        fourths = []
        for at in range(3):
            cols = pl.ds(at * FOURTH, FOURTH)
            fourths.append(tails[kind, :, cols].astype(F32) + tail_lasts[kind, :, cols].astype(F32))
        for at, part in enumerate(unpack(fourths)):
            result[kind, MAIN:OWN, pl.ds(at * FOURTH, FOURTH)] = part[0 : OWN - MAIN].astype(BF16)
    for copy, store in zip(large, stores[2:]):
        copy.wait()
        store.start()
    for copy, store in zip(copies, stores):
        copy.wait()
        store.start()
    for store in stores:
        store.wait()


COPIES = 96


def body(tokens, cotangent, gain, up_weight, down_weight):
    vmem, anywhere = pl.BlockSpec(memory_space=pltpu.VMEM), pl.BlockSpec(memory_space=pl.ANY)
    rows = (1, 4, 2, 2, 32, D)
    main, tail = jax.ShapeDtypeStruct((2, MAIN, D), BF16), jax.ShapeDtypeStruct((2, 16, TAIL), BF16)
    out_shape, gain_shape = jax.ShapeDtypeStruct((32, D), BF16), jax.ShapeDtypeStruct((1, D), F32)
    grad_shape = jax.ShapeDtypeStruct((OWN, D), BF16)
    parts = pl.pallas_call(
        kernel,
        out_shape=(out_shape, gain_shape, main, tail, tail),
        in_specs=[anywhere, anywhere, vmem, anywhere, anywhere],
        out_specs=(anywhere, vmem, anywhere, anywhere, anywhere),
        scratch_shapes=[
            pltpu.VMEM((2, OWN, D), BF16),
            pltpu.VMEM((2, 4, 2, 2, 32, D), BF16),
            pltpu.VMEM((2, 4, 2, 2, 32, D), BF16),
            pltpu.VMEM((2, 4, PAD, D), BF16),
            pltpu.VMEM((2, 4, 16, TAIL), BF16),
            pltpu.VMEM((2 * TOK, 4 * PAD), BF16),
            pltpu.VMEM((4 * PAD, 2 * TOK), BF16),
            pltpu.VMEM((4 * PAD, 2 * TOK), BF16),
            pltpu.VMEM((2, 2 * TOK, 2 * PAD), F32),
            pltpu.VMEM((2, 4, MAIN, D), BF16),
            pltpu.VMEM((2, 4, 16, TAIL), BF16),
            pltpu.VMEM((2, 3, MAIN, D), BF16),
            pltpu.VMEM((2, 2, 16, TAIL), BF16),
            pltpu.VMEM((2, 3, 4, 32, FOURTH), BF16),
            pltpu.VMEM((2, 3, 2, 2, 32, FOURTH), BF16),
            pltpu.VMEM((2, 3, 32, FOURTH), BF16),
            pltpu.VMEM((2, 3, 32, FOURTH), BF16),
            pltpu.VMEM((32, D), BF16),
            pltpu.VMEM((32, D), BF16),
            pltpu.VMEM((8, D), F32),
            pltpu.VMEM((1, D), F32),
            pltpu.VMEM((1, D), F32),
            pltpu.VMEM((1, HALF), F32),
            pltpu.VMEM((2, 1, HALF), F32),
            pltpu.VMEM((3, 4, 1, HALF), F32),
            pltpu.SemaphoreType.DMA((COPIES,)),
            pltpu.SemaphoreType.DMA((COPIES,)),
            pltpu.SemaphoreType.DMA((5,)),
            pltpu.SemaphoreType.DMA((6,)),
            pltpu.SemaphoreType.REGULAR,
        ],
        compiler_params=pltpu.CompilerParams(collective_id=0, has_side_effects=True, vmem_limit_bytes=63 * 2**20),
    )(tokens.reshape(rows), cotangent.reshape(rows), gain[None], up_weight, down_weight)
    out, gain_out, grad_up, grad_down = pl.pallas_call(
        closing_kernel,
        out_shape=(out_shape, gain_shape, grad_shape, grad_shape),
        in_specs=[anywhere] * 5,
        out_specs=(anywhere,) * 4,
        scratch_shapes=[
            pltpu.VMEM((32, D), BF16),
            pltpu.VMEM((1, D), F32),
            pltpu.VMEM((2, 16, TAIL), BF16),
            pltpu.VMEM((2, 16, TAIL), BF16),
            pltpu.VMEM((2, OWN, D), BF16),
            pltpu.SemaphoreType.DMA((8,)),
            pltpu.SemaphoreType.DMA((6,)),
        ],
        compiler_params=pltpu.CompilerParams(vmem_limit_bytes=63 * 2**20),
    )(*parts)
    return (out[None], gain_out[0], grad_up, grad_down)


def solution(mesh):
    placed = (
        P("blk", None, None),
        P("blk", None, None),
        P(),
        P(("dp", "blk"), None),
        P(("dp", "blk"), None),
    )
    return jax.shard_map(
        body,
        mesh=mesh,
        in_specs=placed,
        out_specs=(P("blk", "dp", None), P(), P(("dp", "blk"), None), P(("dp", "blk"), None)),
        check_vma=False,
    )
```

```python
import jax
import jax.numpy as jnp
from jax import lax
from jax.experimental import pallas as pl
from jax.experimental.pallas import tpu as pltpu
from jax.sharding import PartitionSpec as P

D = 5120
TOK = 512
OWN = 108
MAIN = 96
PAD = 128
STEP = 256
HALF = D // 2
FOURTH = D // 4
TAIL = 3 * FOURTH
MESH = pl.DeviceIdType.MESH
BF16 = jnp.bfloat16
F32 = jnp.float32


def columns(step, size=STEP, first=0):
    return pl.ds(pl.multiple_of(first + step * size, size), size)


def row_numbers(like):
    return lax.broadcasted_iota(jnp.int32, like.shape, 0)


def pack(fourth, last, at):
    return jnp.where(row_numbers(fourth) < 12, fourth, pltpu.roll(last, 12 - 4 * at, 0))


def unpack(fourths):
    row = row_numbers(fourths[0])
    moved = [pltpu.roll(fourth, 4 * at + 4, 0) for at, fourth in enumerate(fourths)]
    last = jnp.where(row < 4, moved[0], jnp.where(row < 8, moved[1], jnp.where(row < 12, moved[2], 0.0)))
    return [jnp.where(row < 12, fourth, 0.0) for fourth in fourths] + [last]


def dot(a, b, over):
    return lax.dot_general(a, b, ((over[:1], over[1:]), ((), ())), preferred_element_type=F32)


def kernel(
    tokens_ref, cotangent_ref, gain_ref, up_ref, down_ref,
    out_ref, gain_out_ref, sum_ref, sum_tail_ref, last_tail_ref,
    own, norm, cot, weights, tails, act, act_t, hidden_t, acc, grads, grad_tails, mail, mail_tails,
    x_first, y_first, y_second, x_second,
    own_rows, out_rows, gain_acc, gain_own, gain_other, gain_half, gain_halves, gain_slots, send_sem, recv_sem, local_sem, store_sem, free_sem,
):
    dp, blk = lax.axis_index("dp"), lax.axis_index("blk")
    y, x_lo, core = dp // 4, (dp // 2) % 2, dp % 2
    z, x_hi = blk // 2, blk % 2
    x = 2 * x_hi + x_lo

    def chip(cx, cy, cz, cc):
        return (cy * 4 + (cx % 2) * 2 + cc, cz * 2 + cx // 2)

    def x_at(j):
        return chip((x + j) % 4, y, z, core)

    def y_at(j):
        return chip(x, (y + j) % 4, z, core)

    def z_at(j):
        return chip(x, y, (z + j) % 4, core)

    sibling = chip(x, y, z, 1 - core)
    across = chip(3 - x, y, z, core)
    beside = chip(x + 1 - 2 * x_lo, y, z, core)

    count = [0]

    def send(src, dst, device):
        at = count[0]
        count[0] += 1
        copy = pltpu.make_async_remote_copy(
            src_ref=src, dst_ref=dst, send_sem=send_sem.at[at], recv_sem=recv_sem.at[at], device_id=device, device_id_type=MESH
        )
        copy.start()
        return copy

    loads = [pltpu.make_async_copy(ref, own.at[kind], local_sem.at[3 + kind]) for kind, ref in enumerate((up_ref, down_ref))]
    for load in loads:
        load.start()
    load_tokens = pltpu.make_async_copy(tokens_ref.at[0], norm.at[0], local_sem.at[0])
    load_cot = pltpu.make_async_copy(cotangent_ref.at[0], cot.at[0], local_sem.at[1])
    load_own = pltpu.make_async_copy(tokens_ref.at[0, y, x_lo, core], own_rows, local_sem.at[2])
    load_tokens.start()
    load_cot.start()
    load_own.start()

    partners = [x_at(1), x_at(2), x_at(3), y_at(1), y_at(2), y_at(3), z_at(1), z_at(2), z_at(3), sibling]
    barrier = pltpu.get_barrier_semaphore()
    for partner in partners:
        pl.semaphore_signal(barrier, inc=1, device_id=partner, device_id_type=MESH)

    def fourth_of(at):
        return pl.ds(at * FOURTH, FOURTH)

    pl.semaphore_wait(barrier, len(partners))

    def send_main(kind, to, device):
        return send((up_ref, down_ref)[kind].at[pl.ds(0, MAIN)], weights.at[kind, to, pl.ds(0, MAIN)], device)

    def send_tail(kind, to, device):
        return send(tails.at[kind, 0], tails.at[kind, to], device)

    up_right, down_left = [send_main(0, 2, z_at(1))], [send_main(1, 1, z_at(3))]

    for load in loads:
        load.wait()
    for kind in range(2):
        weights[kind, 0, MAIN:PAD, :] = jnp.zeros((PAD - MAIN, D), BF16)
        weights[kind, 0, MAIN:OWN, :] = own[kind, MAIN:OWN, :]
        last = weights[kind, 0, MAIN : MAIN + 16, fourth_of(3)].astype(F32)
        for at in range(3):
            rows = weights[kind, 0, MAIN : MAIN + 16, fourth_of(at)].astype(F32)
            tails[kind, 0, :, fourth_of(at)] = pack(rows, last, at).astype(BF16)
    up_right.append(send_tail(0, 2, z_at(1)))
    down_left.append(send_tail(1, 1, z_at(3)))
    down_right = [send_main(1, 2, z_at(1)), send_tail(1, 2, z_at(1))]
    up_left = [send_main(0, 1, z_at(3)), send_tail(0, 1, z_at(3))]
    for kind in range(2):
        weights[kind, 0, 0:MAIN, :] = own[kind, 0:MAIN, :]
        for slot in range(1, 4):
            weights[kind, slot, MAIN + 16 : PAD, :] = jnp.zeros((PAD - MAIN - 16, D), BF16)

    def send_block(kind, slot, to, device):
        return [
            send(weights.at[kind, slot, pl.ds(0, MAIN)], weights.at[kind, to, pl.ds(0, MAIN)], device),
            send(tails.at[kind, slot], tails.at[kind, to], device),
        ]

    def wait_recv(copies):
        for copy in copies:
            copy.wait_recv()

    def unpack_block(kind, slot):
        fourths = unpack([tails[kind, slot, :, fourth_of(at)].astype(F32) for at in range(3)])
        for at in range(4):
            weights[kind, slot, MAIN : MAIN + 16, fourth_of(at)] = fourths[at].astype(BF16)

    quarter = (y + 2 * x_lo) % 4
    quarter_across = (y + 2 - 2 * x_lo) % 4

    def piece(ref, which, q):
        return ref.at[which, q, :, core]

    load_cot.wait()
    cot_across = send(piece(cot, 0, quarter_across), piece(cot, 1, quarter_across), across)

    load_tokens.wait()
    gain = gain_ref[...]

    def normalize(step, _):
        at = (0, step // 8, (step // 4) % 2, (step // 2) % 2, pl.ds(pl.multiple_of((step % 2) * 16, 16), 16))
        rows = norm[at].astype(F32)
        inverse = lax.rsqrt(jnp.mean(rows * rows, axis=-1, keepdims=True) + 1e-05)
        norm[at] = (rows * inverse * gain).astype(BF16)
        return 0

    lax.fori_loop(0, 32, normalize, 0)
    norm_across = send(piece(norm, 0, quarter_across), piece(norm, 1, quarter_across), across)

    def forward(slot, blocks, micros):
        width = blocks * PAD
        tall = len(micros) * TOK
        first_row = micros[0] * TOK
        which = slice(micros[0], micros[0] + len(micros))

        for kind, rows in enumerate((norm, cot)):
            left = rows[which].reshape(tall, D)
            right = weights[kind, slot : slot + blocks].reshape(width, D)
            acc[kind, 0:tall, 0:width] = dot(left, right, (1, 1))

        def finish(step, _):
            rows = columns(step, 128)
            hidden, back = acc[0, rows, 0:width], acc[1, rows, 0:width]
            sig = 1.0 / (1.0 + jnp.exp(-hidden))
            active = hidden * sig
            hidden_grad = back * sig * (1.0 + hidden * (1.0 - sig))
            to = columns(step, 128, first_row)
            act[to, slot * PAD : slot * PAD + width] = active.astype(BF16)
            act_t[slot * PAD : slot * PAD + width, to] = active.T.astype(BF16)
            hidden_t[slot * PAD : slot * PAD + width, to] = hidden_grad.T.astype(BF16)
            return 0

        lax.fori_loop(0, tall // 128, finish, 0)

    def backward(slot, blocks, fourth):
        rows = pl.ds(slot * PAD, blocks * PAD)

        at = fourth_of(fourth)
        up_part = dot(hidden_t[rows, :], norm[:, :, :, :, :, at].reshape(2 * TOK, FOURTH), (1, 0))
        terms = weights[0, slot : slot + blocks, :, at].reshape(blocks * PAD, FOURTH).astype(F32) * up_part
        gain_acc[:, at] += jnp.sum(terms.reshape(blocks * PAD // 8, 8, FOURTH), axis=0)
        down_part = dot(act_t[rows, :], cot[:, :, :, :, :, at].reshape(2 * TOK, FOURTH), (1, 0))
        for kind, part in enumerate((up_part, down_part)):
            for b in range(blocks):
                grads[kind, slot + b, :, at] = part[b * PAD : b * PAD + MAIN].astype(BF16)
                end = part[b * PAD + MAIN : b * PAD + MAIN + 16]
                if fourth < 3:
                    grad_tails[kind, slot + b, :, at] = end.astype(BF16)
                    continue
                for other in range(3):
                    to = fourth_of(other)
                    mixed = pack(grad_tails[kind, slot + b, :, to].astype(F32), end, other)
                    grad_tails[kind, slot + b, :, to] = mixed.astype(BF16)

    def send_grads(part, kind, slot, to, device):
        if part == 2:
            target = last_tail_ref.at[kind] if to == 2 else mail_tails.at[kind, to]
            return send(grad_tails.at[kind, slot], target, device)
        at = pl.ds(part * HALF, HALF)
        return send(grads.at[kind, slot, :, at], mail.at[kind, to, :, at], device)

    gain_acc[...] = jnp.zeros_like(gain_acc)
    forward(0, 1, (0,))

    onward = []
    for ref, copy in ((cot, cot_across), (norm, norm_across)):
        copy.wait_recv()
        src = piece(ref, 1, quarter)
        onward.append([send(src, src, device) for device in (beside, y_at(1), y_at(3))] + [send(src, src, sibling)])
    wait_recv(up_right)
    up_relay = send_block(0, 2, 3, z_at(1))
    wait_recv(down_left)
    down_relay = send_block(1, 1, 3, z_at(3))
    shared = []
    for ref, copies in ((cot, onward[0]), (norm, onward[1])):
        for shift, copy in ((2, copies[0]), (3, copies[1]), (1, copies[2])):
            copy.wait_recv()
            src = piece(ref, 1, (quarter + shift) % 4)
            shared.append(send(src, src, sibling))
    for copy in [onward[0][3], onward[1][3]] + shared:
        copy.wait_recv()

    forward(0, 1, (1,))
    wait_recv(down_right)
    wait_recv(up_left)
    for kind in range(2):
        unpack_block(kind, 1)
        unpack_block(kind, 2)
    forward(1, 2, (0, 1))

    direct = []

    def send_direct(part):
        direct.append((send_grads(part, 1, 1, 0, z_at(1)), send_grads(part, 0, 2, 0, z_at(3))))

    for fourth in range(4):
        backward(0, 3, fourth)
        for part in ((), (0,), (), (1, 2))[fourth]:
            send_direct(part)

    wait_recv(up_relay)
    wait_recv(down_relay)
    for kind in range(2):
        unpack_block(kind, 3)
    forward(3, 1, (0, 1))

    for copy in [cot_across, norm_across] + onward[0] + onward[1] + shared:
        copy.wait_send()

    def project(fourth):
        def tile(step, _):
            at = columns(step, STEP, fourth * FOURTH)
            right = weights[1, :, :, at].reshape(4 * PAD, STEP)
            for m in range(2):
                part = dot(act[m * TOK : (m + 1) * TOK, :], right, (1, 0))
                norm[m, :, :, :, :, at] = part.astype(BF16).reshape(4, 2, 2, 32, STEP)
            return 0

        lax.fori_loop(0, FOURTH // STEP, tile, 0)

    def add_core(fourth):
        cols = fourth_of(fourth)

        def tile(step, _):
            at = (step // 8, (step // 2) % 4, step % 2)
            mine = norm[(*at, core, slice(None), cols)].astype(F32)
            theirs = cot[(*at, 0, slice(None), cols)].astype(F32)
            cot[(*at, 0, slice(None), cols)] = (mine + theirs).astype(BF16)
            return 0

        lax.fori_loop(0, 16, tile, 0)

    def microbatch(cx):
        return (cx // 2 + x_hi) % 2

    def first_leg(fourth):
        cores[fourth].wait_recv()
        add_core(fourth)
        cols, turn = fourth_of(fourth), fourth // 2
        copies = []
        for j in range(1, 4):
            to = (x + j) % 4
            if fourth % 2 == 0:
                copies.append(send(cot.at[microbatch(to), :, to % 2, 0, :, cols], x_first.at[turn, j - 1], x_at(j)))
            else:
                copies.append(send(cot.at[:, (y + j) % 4, :, 0, :, cols], y_first.at[turn, j - 1], y_at(j)))
        legs.append(copies)

    def second_leg(fourth):
        for copy in legs[fourth]:
            copy.wait()
        cols, turn = fourth_of(fourth), fourth // 2

        def add(step, _):
            if fourth % 2 == 0:
                total = cot[0, step, x_lo, 0, :, cols].astype(F32)
                for j in range(3):
                    total += x_first[turn, j, step].astype(F32)
                x_first[turn, 0, step] = total.astype(BF16)
            else:
                at = (step // 2, step % 2)
                total = cot[(at[0], y, at[1], 0, slice(None), cols)].astype(F32)
                for j in range(3):
                    total += y_first[(turn, j, *at)].astype(F32)
                y_first[(turn, 0, *at)] = total.astype(BF16)
            return 0

        lax.fori_loop(0, 4, add, 0)
        copies = []
        for j in range(1, 4):
            to = (x + j) % 4
            if fourth % 2 == 0:
                copies.append(send(x_first.at[turn, 0, (y + j) % 4], y_second.at[turn, j - 1], y_at(j)))
            else:
                copies.append(send(y_first.at[turn, 0, microbatch(to), to % 2], x_second.at[turn, j - 1], x_at(j)))
        legs[fourth] = copies

    def last_sum(fourth):
        for copy in legs[fourth]:
            copy.wait()
        cols, turn = fourth_of(fourth), fourth // 2
        if fourth % 2 == 0:
            total, others = x_first[turn, 0, y], y_second
        else:
            total, others = y_first[turn, 0, 0, x_lo], x_second
        total = own_rows[:, cols].astype(F32) + total.astype(F32)
        for j in range(3):
            total += others[turn, j].astype(F32)
        out_rows[:, cols] = total.astype(BF16)

    far, cores, legs = [], [], []

    def send_far(part):
        far.append((send_grads(part, 0, 3, 1, z_at(1)), send_grads(part, 1, 3, 1, z_at(3))))

    def share(fourth):
        project(fourth)
        pl.semaphore_wait(free_sem, 1)
        cols = fourth_of(fourth)
        cores.append(send(norm.at[:, :, :, 1 - core, :, cols], cot.at[:, :, :, 0, :, cols], sibling))

    for fourth in range(4):
        backward(3, 1, fourth)
        pl.semaphore_signal(free_sem, inc=1, device_id=sibling, device_id_type=MESH)
        if fourth == 1:
            send_far(0)
            share(0)
        if fourth == 3:
            send_far(1)
            send_far(2)
    for fourth in range(1, 4):
        share(fourth)
        first_leg(fourth - 1)
    gain_own[...] = jnp.sum(gain_acc[...], axis=0, keepdims=True)
    gain_core = send(gain_own, gain_other, sibling)
    first_leg(3)

    def spread(stage, place, others):
        gain_slots[stage, place] = gain_half[...]
        return [send(gain_half, gain_slots.at[stage, place], other) for other in others]

    def gather(stage, copies):
        for copy in copies:
            copy.wait()
        gain_half[...] = (gain_slots[stage, 0] + gain_slots[stage, 1]) + (gain_slots[stage, 2] + gain_slots[stage, 3])

    gain_core.wait()
    own_half = pl.ds(pl.multiple_of(core * HALF, HALF), HALF)
    gain_half[...] = gain_own[:, own_half] + gain_other[:, own_half]
    gain_z = spread(0, z, [z_at(j) for j in range(1, 4)])

    last_leg = []

    def combine(part):
        for copy in far[part]:
            copy.wait_recv()
        pairs = ((0, 1), (1, 2))
        if part == 2:
            for kind, slot in pairs:
                total = grad_tails[kind, slot].astype(F32) + mail_tails[kind, 1].astype(F32)
                grad_tails[kind, slot] = total.astype(BF16)
        else:

            def tile(step, _):
                cols = columns(step, 512, part * HALF)
                for kind, slot in pairs:
                    total = grads[kind, slot, :, cols].astype(F32) + mail[kind, 1, :, cols].astype(F32)
                    grads[kind, slot, :, cols] = total.astype(BF16)
                return 0

            lax.fori_loop(0, HALF // 512, tile, 0)
        last_leg.append((send_grads(part, 0, 1, 2, z_at(1)), send_grads(part, 1, 2, 2, z_at(3))))

    second_leg(0)
    second_leg(1)
    combine(0)
    second_leg(2)
    combine(1)
    combine(2)
    second_leg(3)

    load_own.wait()
    gather(0, gain_z)
    gain_x = spread(1, x, [x_at(j) for j in range(1, 4)])
    last_sum(0)
    last_sum(1)
    gather(1, gain_x)
    gain_y = spread(2, y, [y_at(j) for j in range(1, 4)])
    last_sum(2)
    last_sum(3)
    gather(2, gain_y)
    gain_last = send(gain_half, gain_halves.at[core], sibling)
    gain_halves[core] = gain_half[...]

    stores = [pltpu.make_async_copy(out_rows, out_ref, local_sem.at[0])]
    stores[0].start()

    def store(src, dst):
        stores.append(pltpu.make_async_copy(src, dst, store_sem.at[len(stores) - 1]))
        stores[-1].start()

    for copy in direct[2]:
        copy.wait_recv()
    for kind in range(2):
        total = grad_tails[kind, 0].astype(F32) + mail_tails[kind, 0].astype(F32)
        grad_tails[kind, 0] = total.astype(BF16)
        store(grad_tails.at[kind, 0], sum_tail_ref.at[kind])
    gain_last.wait()
    for at in range(2):
        cols = pl.ds(at * HALF, HALF)
        gain_out_ref[:, cols] = gain_halves[at] / gain_ref[:, cols]
    for part in range(2):
        for copy in (*direct[part], *last_leg[part]):
            copy.wait_recv()

        def finish(step, _):
            cols = columns(step, 512, part * HALF)
            for kind in range(2):
                total = grads[kind, 0, :, cols].astype(F32)
                total += mail[kind, 0, :, cols].astype(F32)
                total += mail[kind, 2, :, cols].astype(F32)
                grads[kind, 0, :, cols] = total.astype(BF16)
            return 0

        lax.fori_loop(0, HALF // 512, finish, 0)
        for kind in range(2):
            at = pl.ds(part * HALF, HALF)
            store(grads.at[kind, 0, :, at], sum_ref.at[kind, :, at])
    for copy in last_leg[2]:
        copy.wait_recv()
    for copy in stores:
        copy.wait()

    for copies in (up_right, down_left, down_right, up_left, up_relay, down_relay, cores, *direct, *far, *last_leg):
        for copy in copies:
            copy.wait_send()


def closing_kernel(
    rows_ref, gain_ref, sum_ref, sum_tail_ref, last_tail_ref, out_ref, gain_out_ref, grad_up_ref, grad_down_ref,
    rows, gain, tails, tail_lasts, result, load_sem, store_sem,
):
    loads = []

    def load(src, dst):
        loads.append(pltpu.make_async_copy(src, dst, load_sem.at[len(loads)]))
        loads[-1].start()
        return loads[-1]

    small = [load(sum_tail_ref, tails), load(last_tail_ref, tail_lasts)]
    pieces = [(kind, pl.ds(part * HALF, HALF)) for kind in range(2) for part in range(2)]
    large = [load(sum_ref.at[kind, :, at], result.at[kind, pl.ds(0, MAIN), at]) for kind, at in pieces]
    copies = [load(rows_ref, rows), load(gain_ref, gain)]
    stores = [
        pltpu.make_async_copy(rows, out_ref, store_sem.at[0]),
        pltpu.make_async_copy(gain, gain_out_ref, store_sem.at[1]),
    ]
    for index, (kind, at) in enumerate(pieces):
        target = (grad_up_ref, grad_down_ref)[kind].at[:, at]
        stores.append(pltpu.make_async_copy(result.at[kind, :, at], target, store_sem.at[2 + index]))
    for copy in small:
        copy.wait()
    for kind in range(2):
        fourths = []
        for at in range(3):
            cols = pl.ds(at * FOURTH, FOURTH)
            fourths.append(tails[kind, :, cols].astype(F32) + tail_lasts[kind, :, cols].astype(F32))
        for at, part in enumerate(unpack(fourths)):
            result[kind, MAIN:OWN, pl.ds(at * FOURTH, FOURTH)] = part[0 : OWN - MAIN].astype(BF16)
    for copy, store in zip(large, stores[2:]):
        copy.wait()
        store.start()
    for copy, store in zip(copies, stores):
        copy.wait()
        store.start()
    for store in stores:
        store.wait()


COPIES = 96


def body(tokens, cotangent, gain, up_weight, down_weight):
    vmem, anywhere = pl.BlockSpec(memory_space=pltpu.VMEM), pl.BlockSpec(memory_space=pl.ANY)
    rows = (1, 4, 2, 2, 32, D)
    main, tail = jax.ShapeDtypeStruct((2, MAIN, D), BF16), jax.ShapeDtypeStruct((2, 16, TAIL), BF16)
    out_shape, gain_shape = jax.ShapeDtypeStruct((32, D), BF16), jax.ShapeDtypeStruct((1, D), F32)
    grad_shape = jax.ShapeDtypeStruct((OWN, D), BF16)
    parts = pl.pallas_call(
        kernel,
        out_shape=(out_shape, gain_shape, main, tail, tail),
        in_specs=[anywhere, anywhere, vmem, anywhere, anywhere],
        out_specs=(anywhere, vmem, anywhere, anywhere, anywhere),
        scratch_shapes=[
            pltpu.VMEM((2, OWN, D), BF16),
            pltpu.VMEM((2, 4, 2, 2, 32, D), BF16),
            pltpu.VMEM((2, 4, 2, 2, 32, D), BF16),
            pltpu.VMEM((2, 4, PAD, D), BF16),
            pltpu.VMEM((2, 4, 16, TAIL), BF16),
            pltpu.VMEM((2 * TOK, 4 * PAD), BF16),
            pltpu.VMEM((4 * PAD, 2 * TOK), BF16),
            pltpu.VMEM((4 * PAD, 2 * TOK), BF16),
            pltpu.VMEM((2, 2 * TOK, 2 * PAD), F32),
            pltpu.VMEM((2, 4, MAIN, D), BF16),
            pltpu.VMEM((2, 4, 16, TAIL), BF16),
            pltpu.VMEM((2, 3, MAIN, D), BF16),
            pltpu.VMEM((2, 2, 16, TAIL), BF16),
            pltpu.VMEM((2, 3, 4, 32, FOURTH), BF16),
            pltpu.VMEM((2, 3, 2, 2, 32, FOURTH), BF16),
            pltpu.VMEM((2, 3, 32, FOURTH), BF16),
            pltpu.VMEM((2, 3, 32, FOURTH), BF16),
            pltpu.VMEM((32, D), BF16),
            pltpu.VMEM((32, D), BF16),
            pltpu.VMEM((8, D), F32),
            pltpu.VMEM((1, D), F32),
            pltpu.VMEM((1, D), F32),
            pltpu.VMEM((1, HALF), F32),
            pltpu.VMEM((2, 1, HALF), F32),
            pltpu.VMEM((3, 4, 1, HALF), F32),
            pltpu.SemaphoreType.DMA((COPIES,)),
            pltpu.SemaphoreType.DMA((COPIES,)),
            pltpu.SemaphoreType.DMA((5,)),
            pltpu.SemaphoreType.DMA((6,)),
            pltpu.SemaphoreType.REGULAR,
        ],
        compiler_params=pltpu.CompilerParams(collective_id=0, has_side_effects=True, vmem_limit_bytes=63 * 2**20),
    )(tokens.reshape(rows), cotangent.reshape(rows), gain[None], up_weight, down_weight)
    out, gain_out, grad_up, grad_down = pl.pallas_call(
        closing_kernel,
        out_shape=(out_shape, gain_shape, grad_shape, grad_shape),
        in_specs=[anywhere] * 5,
        out_specs=(anywhere,) * 4,
        scratch_shapes=[
            pltpu.VMEM((32, D), BF16),
            pltpu.VMEM((1, D), F32),
            pltpu.VMEM((2, 16, TAIL), BF16),
            pltpu.VMEM((2, 16, TAIL), BF16),
            pltpu.VMEM((2, OWN, D), BF16),
            pltpu.SemaphoreType.DMA((8,)),
            pltpu.SemaphoreType.DMA((6,)),
        ],
        compiler_params=pltpu.CompilerParams(vmem_limit_bytes=63 * 2**20),
    )(*parts)
    return (out[None], gain_out[0], grad_up, grad_down)


def solution(mesh):
    placed = (
        P("blk", None, None),
        P("blk", None, None),
        P(),
        P(("dp", "blk"), None),
        P(("dp", "blk"), None),
    )
    return jax.shard_map(
        body,
        mesh=mesh,
        in_specs=placed,
        out_specs=(P("blk", "dp", None), P(), P(("dp", "blk"), None), P(("dp", "blk"), None)),
        check_vma=False,
    )
```

```python
import jax
import jax.numpy as jnp
from jax import lax
from jax.experimental import pallas as pl
from jax.experimental.pallas import tpu as pltpu
from jax.sharding import PartitionSpec as P

D = 5120
TOK = 512
OWN = 108
MAIN = 96
PAD = 128
STEP = 256
HALF = D // 2
FOURTH = D // 4
TAIL = 3 * FOURTH
MESH = pl.DeviceIdType.MESH
BF16 = jnp.bfloat16
F32 = jnp.float32


def columns(step, size=STEP, first=0):
    return pl.ds(pl.multiple_of(first + step * size, size), size)


def row_numbers(like):
    return lax.broadcasted_iota(jnp.int32, like.shape, 0)


def pack(fourth, last, at):
    return jnp.where(row_numbers(fourth) < 12, fourth, pltpu.roll(last, 12 - 4 * at, 0))


def unpack(fourths):
    row = row_numbers(fourths[0])
    moved = [pltpu.roll(fourth, 4 * at + 4, 0) for at, fourth in enumerate(fourths)]
    last = jnp.where(row < 4, moved[0], jnp.where(row < 8, moved[1], jnp.where(row < 12, moved[2], 0.0)))
    return [jnp.where(row < 12, fourth, 0.0) for fourth in fourths] + [last]


def dot(a, b, over):
    return lax.dot_general(a, b, ((over[:1], over[1:]), ((), ())), preferred_element_type=F32)


def kernel(
    tokens_ref, cotangent_ref, gain_ref, up_ref, down_ref,
    out_ref, gain_out_ref, sum_ref, sum_tail_ref, last_tail_ref,
    own, norm, cot, weights, tails, act, act_t, hidden_t, acc, grads, grad_tails, mail, mail_tails,
    x_first, y_first, y_second, x_second,
    own_rows, out_rows, gain_acc, gain_own, gain_other, gain_half, gain_halves, gain_slots, send_sem, recv_sem, local_sem, store_sem, free_sem,
):
    dp, blk = lax.axis_index("dp"), lax.axis_index("blk")
    y, x_lo, core = dp // 4, (dp // 2) % 2, dp % 2
    z, x_hi = blk // 2, blk % 2
    x = 2 * x_hi + x_lo

    def chip(cx, cy, cz, cc):
        return (cy * 4 + (cx % 2) * 2 + cc, cz * 2 + cx // 2)

    def x_at(j):
        return chip((x + j) % 4, y, z, core)

    def y_at(j):
        return chip(x, (y + j) % 4, z, core)

    def z_at(j):
        return chip(x, y, (z + j) % 4, core)

    sibling = chip(x, y, z, 1 - core)
    across = chip(3 - x, y, z, core)
    beside = chip(x + 1 - 2 * x_lo, y, z, core)

    count = [0]

    def send(src, dst, device):
        at = count[0]
        count[0] += 1
        copy = pltpu.make_async_remote_copy(
            src_ref=src, dst_ref=dst, send_sem=send_sem.at[at], recv_sem=recv_sem.at[at], device_id=device, device_id_type=MESH
        )
        copy.start()
        return copy

    loads = [pltpu.make_async_copy(ref, own.at[kind], local_sem.at[3 + kind]) for kind, ref in enumerate((up_ref, down_ref))]
    for load in loads:
        load.start()
    load_tokens = pltpu.make_async_copy(tokens_ref.at[0], norm.at[0], local_sem.at[0])
    load_cot = pltpu.make_async_copy(cotangent_ref.at[0], cot.at[0], local_sem.at[1])
    load_own = pltpu.make_async_copy(tokens_ref.at[0, y, x_lo, core], own_rows, local_sem.at[2])
    load_tokens.start()
    load_cot.start()
    load_own.start()

    partners = [x_at(1), x_at(2), x_at(3), y_at(1), y_at(2), y_at(3), z_at(1), z_at(2), z_at(3), sibling]
    barrier = pltpu.get_barrier_semaphore()
    for partner in partners:
        pl.semaphore_signal(barrier, inc=1, device_id=partner, device_id_type=MESH)

    def fourth_of(at):
        return pl.ds(at * FOURTH, FOURTH)

    pl.semaphore_wait(barrier, len(partners))

    def send_main(kind, to, device):
        return send((up_ref, down_ref)[kind].at[pl.ds(0, MAIN)], weights.at[kind, to, pl.ds(0, MAIN)], device)

    def send_tail(kind, to, device):
        return send(tails.at[kind, 0], tails.at[kind, to], device)

    up_right, down_left = [send_main(0, 2, z_at(1))], [send_main(1, 1, z_at(3))]

    for load in loads:
        load.wait()
    for kind in range(2):
        weights[kind, 0, MAIN:PAD, :] = jnp.zeros((PAD - MAIN, D), BF16)
        weights[kind, 0, MAIN:OWN, :] = own[kind, MAIN:OWN, :]
        last = weights[kind, 0, MAIN : MAIN + 16, fourth_of(3)].astype(F32)
        for at in range(3):
            rows = weights[kind, 0, MAIN : MAIN + 16, fourth_of(at)].astype(F32)
            tails[kind, 0, :, fourth_of(at)] = pack(rows, last, at).astype(BF16)
    up_right.append(send_tail(0, 2, z_at(1)))
    down_left.append(send_tail(1, 1, z_at(3)))
    down_right = [send_main(1, 2, z_at(1)), send_tail(1, 2, z_at(1))]
    up_left = [send_main(0, 1, z_at(3)), send_tail(0, 1, z_at(3))]
    for kind in range(2):
        weights[kind, 0, 0:MAIN, :] = own[kind, 0:MAIN, :]
        for slot in range(1, 4):
            weights[kind, slot, MAIN + 16 : PAD, :] = jnp.zeros((PAD - MAIN - 16, D), BF16)

    def send_block(kind, slot, to, device):
        return [
            send(weights.at[kind, slot, pl.ds(0, MAIN)], weights.at[kind, to, pl.ds(0, MAIN)], device),
            send(tails.at[kind, slot], tails.at[kind, to], device),
        ]

    def wait_recv(copies):
        for copy in copies:
            copy.wait_recv()

    def unpack_block(kind, slot):
        fourths = unpack([tails[kind, slot, :, fourth_of(at)].astype(F32) for at in range(3)])
        for at in range(4):
            weights[kind, slot, MAIN : MAIN + 16, fourth_of(at)] = fourths[at].astype(BF16)

    quarter = (y + 2 * x_lo) % 4
    quarter_across = (y + 2 - 2 * x_lo) % 4

    def piece(ref, which, q):
        return ref.at[which, q, :, core]

    load_cot.wait()
    cot_across = send(piece(cot, 0, quarter_across), piece(cot, 1, quarter_across), across)

    load_tokens.wait()
    gain = gain_ref[...]

    def normalize(step, _):
        at = (0, step // 8, (step // 4) % 2, (step // 2) % 2, pl.ds(pl.multiple_of((step % 2) * 16, 16), 16))
        rows = norm[at].astype(F32)
        inverse = lax.rsqrt(jnp.mean(rows * rows, axis=-1, keepdims=True) + 1e-05)
        norm[at] = (rows * inverse * gain).astype(BF16)
        return 0

    lax.fori_loop(0, 32, normalize, 0)
    norm_across = send(piece(norm, 0, quarter_across), piece(norm, 1, quarter_across), across)

    def forward(slot, blocks, micros):
        width = blocks * PAD
        tall = len(micros) * TOK
        first_row = micros[0] * TOK
        which = slice(micros[0], micros[0] + len(micros))

        for kind, rows in enumerate((norm, cot)):
            left = rows[which].reshape(tall, D)
            right = weights[kind, slot : slot + blocks].reshape(width, D)
            acc[kind, 0:tall, 0:width] = dot(left, right, (1, 1))

        def finish(step, _):
            rows = columns(step, 128)
            hidden, back = acc[0, rows, 0:width], acc[1, rows, 0:width]
            sig = 1.0 / (1.0 + jnp.exp(-hidden))
            active = hidden * sig
            hidden_grad = back * sig * (1.0 + hidden * (1.0 - sig))
            to = columns(step, 128, first_row)
            act[to, slot * PAD : slot * PAD + width] = active.astype(BF16)
            act_t[slot * PAD : slot * PAD + width, to] = active.T.astype(BF16)
            hidden_t[slot * PAD : slot * PAD + width, to] = hidden_grad.T.astype(BF16)
            return 0

        lax.fori_loop(0, tall // 128, finish, 0)

    def backward(slot, blocks, fourth):
        rows = pl.ds(slot * PAD, blocks * PAD)

        at = fourth_of(fourth)
        up_part = dot(hidden_t[rows, :], norm[:, :, :, :, :, at].reshape(2 * TOK, FOURTH), (1, 0))
        terms = weights[0, slot : slot + blocks, :, at].reshape(blocks * PAD, FOURTH).astype(F32) * up_part
        gain_acc[:, at] += jnp.sum(terms.reshape(blocks * PAD // 8, 8, FOURTH), axis=0)
        down_part = dot(act_t[rows, :], cot[:, :, :, :, :, at].reshape(2 * TOK, FOURTH), (1, 0))
        for kind, part in enumerate((up_part, down_part)):
            for b in range(blocks):
                grads[kind, slot + b, :, at] = part[b * PAD : b * PAD + MAIN].astype(BF16)
                end = part[b * PAD + MAIN : b * PAD + MAIN + 16]
                if fourth < 3:
                    grad_tails[kind, slot + b, :, at] = end.astype(BF16)
                    continue
                for other in range(3):
                    to = fourth_of(other)
                    mixed = pack(grad_tails[kind, slot + b, :, to].astype(F32), end, other)
                    grad_tails[kind, slot + b, :, to] = mixed.astype(BF16)

    def send_grads(part, kind, slot, to, device):
        if part == 2:
            target = last_tail_ref.at[kind] if to == 2 else mail_tails.at[kind, to]
            return send(grad_tails.at[kind, slot], target, device)
        at = pl.ds(part * HALF, HALF)
        return send(grads.at[kind, slot, :, at], mail.at[kind, to, :, at], device)

    gain_acc[...] = jnp.zeros_like(gain_acc)
    forward(0, 1, (0,))

    onward = []
    for ref, copy in ((cot, cot_across), (norm, norm_across)):
        copy.wait_recv()
        src = piece(ref, 1, quarter)
        onward.append([send(src, src, device) for device in (beside, y_at(1), y_at(3))] + [send(src, src, sibling)])
    wait_recv(up_right)
    up_relay = send_block(0, 2, 3, z_at(1))
    wait_recv(down_left)
    down_relay = send_block(1, 1, 3, z_at(3))
    shared = []
    for ref, copies in ((cot, onward[0]), (norm, onward[1])):
        for shift, copy in ((2, copies[0]), (3, copies[1]), (1, copies[2])):
            copy.wait_recv()
            src = piece(ref, 1, (quarter + shift) % 4)
            shared.append(send(src, src, sibling))
    for copy in [onward[0][3], onward[1][3]] + shared:
        copy.wait_recv()

    forward(0, 1, (1,))
    wait_recv(down_right)
    wait_recv(up_left)
    for kind in range(2):
        unpack_block(kind, 1)
        unpack_block(kind, 2)
    forward(1, 2, (0, 1))

    direct = []

    def send_direct(part):
        direct.append((send_grads(part, 1, 1, 0, z_at(1)), send_grads(part, 0, 2, 0, z_at(3))))

    for fourth in range(4):
        backward(0, 3, fourth)
        for part in ((), (0,), (), (1, 2))[fourth]:
            send_direct(part)

    wait_recv(up_relay)
    wait_recv(down_relay)
    for kind in range(2):
        unpack_block(kind, 3)
    forward(3, 1, (0, 1))

    for copy in [cot_across, norm_across] + onward[0] + onward[1] + shared:
        copy.wait_send()

    def project(fourth):
        def tile(step, _):
            at = columns(step, STEP, fourth * FOURTH)
            right = weights[1, :, :, at].reshape(4 * PAD, STEP)
            for m in range(2):
                part = dot(act[m * TOK : (m + 1) * TOK, :], right, (1, 0))
                norm[m, :, :, :, :, at] = part.astype(BF16).reshape(4, 2, 2, 32, STEP)
            return 0

        lax.fori_loop(0, FOURTH // STEP, tile, 0)

    def add_core(fourth):
        cols = fourth_of(fourth)

        def tile(step, _):
            at = (step // 8, (step // 2) % 4, step % 2)
            mine = norm[(*at, core, slice(None), cols)].astype(F32)
            theirs = cot[(*at, 0, slice(None), cols)].astype(F32)
            cot[(*at, 0, slice(None), cols)] = (mine + theirs).astype(BF16)
            return 0

        lax.fori_loop(0, 16, tile, 0)

    def microbatch(cx):
        return (cx // 2 + x_hi) % 2

    def first_leg(fourth):
        cores[fourth].wait_recv()
        add_core(fourth)
        cols, turn = fourth_of(fourth), fourth // 2
        copies = []
        for j in range(1, 4):
            to = (x + j) % 4
            if fourth % 2 == 0:
                copies.append(send(cot.at[microbatch(to), :, to % 2, 0, :, cols], x_first.at[turn, j - 1], x_at(j)))
            else:
                copies.append(send(cot.at[:, (y + j) % 4, :, 0, :, cols], y_first.at[turn, j - 1], y_at(j)))
        legs.append(copies)

    def second_leg(fourth):
        for copy in legs[fourth]:
            copy.wait()
        cols, turn = fourth_of(fourth), fourth // 2

        def add(step, _):
            if fourth % 2 == 0:
                total = cot[0, step, x_lo, 0, :, cols].astype(F32)
                for j in range(3):
                    total += x_first[turn, j, step].astype(F32)
                x_first[turn, 0, step] = total.astype(BF16)
            else:
                at = (step // 2, step % 2)
                total = cot[(at[0], y, at[1], 0, slice(None), cols)].astype(F32)
                for j in range(3):
                    total += y_first[(turn, j, *at)].astype(F32)
                y_first[(turn, 0, *at)] = total.astype(BF16)
            return 0

        lax.fori_loop(0, 4, add, 0)
        copies = []
        for j in range(1, 4):
            to = (x + j) % 4
            if fourth % 2 == 0:
                copies.append(send(x_first.at[turn, 0, (y + j) % 4], y_second.at[turn, j - 1], y_at(j)))
            else:
                copies.append(send(y_first.at[turn, 0, microbatch(to), to % 2], x_second.at[turn, j - 1], x_at(j)))
        legs[fourth] = copies

    def last_sum(fourth):
        for copy in legs[fourth]:
            copy.wait()
        cols, turn = fourth_of(fourth), fourth // 2
        if fourth % 2 == 0:
            total, others = x_first[turn, 0, y], y_second
        else:
            total, others = y_first[turn, 0, 0, x_lo], x_second
        total = own_rows[:, cols].astype(F32) + total.astype(F32)
        for j in range(3):
            total += others[turn, j].astype(F32)
        out_rows[:, cols] = total.astype(BF16)

    far, cores, legs = [], [], []

    def send_far(part):
        far.append((send_grads(part, 0, 3, 1, z_at(1)), send_grads(part, 1, 3, 1, z_at(3))))

    def share(fourth):
        project(fourth)
        pl.semaphore_wait(free_sem, 1)
        cols = fourth_of(fourth)
        cores.append(send(norm.at[:, :, :, 1 - core, :, cols], cot.at[:, :, :, 0, :, cols], sibling))

    for fourth in range(4):
        backward(3, 1, fourth)
        pl.semaphore_signal(free_sem, inc=1, device_id=sibling, device_id_type=MESH)
        if fourth == 1:
            send_far(0)
            share(0)
        if fourth == 3:
            send_far(1)
            send_far(2)
    for fourth in range(1, 4):
        share(fourth)
        first_leg(fourth - 1)
    gain_own[...] = jnp.sum(gain_acc[...], axis=0, keepdims=True)
    gain_core = send(gain_own, gain_other, sibling)
    first_leg(3)

    def spread(stage, place, others):
        gain_slots[stage, place] = gain_half[...]
        return [send(gain_half, gain_slots.at[stage, place], other) for other in others]

    def gather(stage, copies):
        for copy in copies:
            copy.wait()
        gain_half[...] = (gain_slots[stage, 0] + gain_slots[stage, 1]) + (gain_slots[stage, 2] + gain_slots[stage, 3])

    gain_core.wait()
    own_half = pl.ds(pl.multiple_of(core * HALF, HALF), HALF)
    gain_half[...] = gain_own[:, own_half] + gain_other[:, own_half]
    gain_z = spread(0, z, [z_at(j) for j in range(1, 4)])

    last_leg = []

    def combine(part):
        for copy in far[part]:
            copy.wait_recv()
        pairs = ((0, 1), (1, 2))
        if part == 2:
            for kind, slot in pairs:
                total = grad_tails[kind, slot].astype(F32) + mail_tails[kind, 1].astype(F32)
                grad_tails[kind, slot] = total.astype(BF16)
        else:

            def tile(step, _):
                cols = columns(step, 512, part * HALF)
                for kind, slot in pairs:
                    total = grads[kind, slot, :, cols].astype(F32) + mail[kind, 1, :, cols].astype(F32)
                    grads[kind, slot, :, cols] = total.astype(BF16)
                return 0

            lax.fori_loop(0, HALF // 512, tile, 0)
        last_leg.append((send_grads(part, 0, 1, 2, z_at(1)), send_grads(part, 1, 2, 2, z_at(3))))

    second_leg(0)
    second_leg(1)
    combine(0)
    second_leg(2)
    combine(1)
    combine(2)
    second_leg(3)

    load_own.wait()
    gather(0, gain_z)
    gain_x = spread(1, x, [x_at(j) for j in range(1, 4)])
    last_sum(0)
    last_sum(1)
    gather(1, gain_x)
    gain_y = spread(2, y, [y_at(j) for j in range(1, 4)])
    last_sum(2)
    last_sum(3)
    gather(2, gain_y)
    gain_last = send(gain_half, gain_halves.at[core], sibling)
    gain_halves[core] = gain_half[...]

    stores = [pltpu.make_async_copy(out_rows, out_ref, local_sem.at[0])]
    stores[0].start()

    def store(src, dst):
        stores.append(pltpu.make_async_copy(src, dst, store_sem.at[len(stores) - 1]))
        stores[-1].start()

    for copy in direct[2]:
        copy.wait_recv()
    for kind in range(2):
        total = grad_tails[kind, 0].astype(F32) + mail_tails[kind, 0].astype(F32)
        grad_tails[kind, 0] = total.astype(BF16)
        store(grad_tails.at[kind, 0], sum_tail_ref.at[kind])
    gain_last.wait()
    for at in range(2):
        cols = pl.ds(at * HALF, HALF)
        gain_out_ref[:, cols] = gain_halves[at] / gain_ref[:, cols]
    for part in range(2):
        for copy in (*direct[part], *last_leg[part]):
            copy.wait_recv()

        def finish(step, _):
            cols = columns(step, 512, part * HALF)
            for kind in range(2):
                total = grads[kind, 0, :, cols].astype(F32)
                total += mail[kind, 0, :, cols].astype(F32)
                total += mail[kind, 2, :, cols].astype(F32)
                grads[kind, 0, :, cols] = total.astype(BF16)
            return 0

        lax.fori_loop(0, HALF // 512, finish, 0)
        for kind in range(2):
            at = pl.ds(part * HALF, HALF)
            store(grads.at[kind, 0, :, at], sum_ref.at[kind, :, at])
    for copy in last_leg[2]:
        copy.wait_recv()
    for copy in stores:
        copy.wait()

    for copies in (up_right, down_left, down_right, up_left, up_relay, down_relay, cores, *direct, *far, *last_leg):
        for copy in copies:
            copy.wait_send()


def closing_kernel(
    rows_ref, gain_ref, sum_ref, sum_tail_ref, last_tail_ref, out_ref, gain_out_ref, grad_up_ref, grad_down_ref,
    rows, gain, tails, tail_lasts, result, load_sem, store_sem,
):
    loads = []

    def load(src, dst):
        loads.append(pltpu.make_async_copy(src, dst, load_sem.at[len(loads)]))
        loads[-1].start()
        return loads[-1]

    small = [load(sum_tail_ref, tails), load(last_tail_ref, tail_lasts)]
    pieces = [(kind, pl.ds(part * FOURTH, FOURTH)) for kind in range(2) for part in range(4)]
    large = [load(sum_ref.at[kind, :, at], result.at[kind, pl.ds(0, MAIN), at]) for kind, at in pieces]
    copies = [load(rows_ref, rows), load(gain_ref, gain)]
    stores = [
        pltpu.make_async_copy(rows, out_ref, store_sem.at[0]),
        pltpu.make_async_copy(gain, gain_out_ref, store_sem.at[1]),
    ]
    for index, (kind, at) in enumerate(pieces):
        target = (grad_up_ref, grad_down_ref)[kind].at[:, at]
        stores.append(pltpu.make_async_copy(result.at[kind, :, at], target, store_sem.at[2 + index]))
    for copy in small:
        copy.wait()
    for kind in range(2):
        fourths = []
        for at in range(3):
            cols = pl.ds(at * FOURTH, FOURTH)
            fourths.append(tails[kind, :, cols].astype(F32) + tail_lasts[kind, :, cols].astype(F32))
        for at, part in enumerate(unpack(fourths)):
            result[kind, MAIN:OWN, pl.ds(at * FOURTH, FOURTH)] = part[0 : OWN - MAIN].astype(BF16)
    for copy, store in zip(large, stores[2:]):
        copy.wait()
        store.start()
    for copy, store in zip(copies, stores):
        copy.wait()
        store.start()
    for store in stores:
        store.wait()


COPIES = 96


def body(tokens, cotangent, gain, up_weight, down_weight):
    vmem, anywhere = pl.BlockSpec(memory_space=pltpu.VMEM), pl.BlockSpec(memory_space=pl.ANY)
    rows = (1, 4, 2, 2, 32, D)
    main, tail = jax.ShapeDtypeStruct((2, MAIN, D), BF16), jax.ShapeDtypeStruct((2, 16, TAIL), BF16)
    out_shape, gain_shape = jax.ShapeDtypeStruct((32, D), BF16), jax.ShapeDtypeStruct((1, D), F32)
    grad_shape = jax.ShapeDtypeStruct((OWN, D), BF16)
    parts = pl.pallas_call(
        kernel,
        out_shape=(out_shape, gain_shape, main, tail, tail),
        in_specs=[anywhere, anywhere, vmem, anywhere, anywhere],
        out_specs=(anywhere, vmem, anywhere, anywhere, anywhere),
        scratch_shapes=[
            pltpu.VMEM((2, OWN, D), BF16),
            pltpu.VMEM((2, 4, 2, 2, 32, D), BF16),
            pltpu.VMEM((2, 4, 2, 2, 32, D), BF16),
            pltpu.VMEM((2, 4, PAD, D), BF16),
            pltpu.VMEM((2, 4, 16, TAIL), BF16),
            pltpu.VMEM((2 * TOK, 4 * PAD), BF16),
            pltpu.VMEM((4 * PAD, 2 * TOK), BF16),
            pltpu.VMEM((4 * PAD, 2 * TOK), BF16),
            pltpu.VMEM((2, 2 * TOK, 2 * PAD), F32),
            pltpu.VMEM((2, 4, MAIN, D), BF16),
            pltpu.VMEM((2, 4, 16, TAIL), BF16),
            pltpu.VMEM((2, 3, MAIN, D), BF16),
            pltpu.VMEM((2, 2, 16, TAIL), BF16),
            pltpu.VMEM((2, 3, 4, 32, FOURTH), BF16),
            pltpu.VMEM((2, 3, 2, 2, 32, FOURTH), BF16),
            pltpu.VMEM((2, 3, 32, FOURTH), BF16),
            pltpu.VMEM((2, 3, 32, FOURTH), BF16),
            pltpu.VMEM((32, D), BF16),
            pltpu.VMEM((32, D), BF16),
            pltpu.VMEM((8, D), F32),
            pltpu.VMEM((1, D), F32),
            pltpu.VMEM((1, D), F32),
            pltpu.VMEM((1, HALF), F32),
            pltpu.VMEM((2, 1, HALF), F32),
            pltpu.VMEM((3, 4, 1, HALF), F32),
            pltpu.SemaphoreType.DMA((COPIES,)),
            pltpu.SemaphoreType.DMA((COPIES,)),
            pltpu.SemaphoreType.DMA((5,)),
            pltpu.SemaphoreType.DMA((6,)),
            pltpu.SemaphoreType.REGULAR,
        ],
        compiler_params=pltpu.CompilerParams(collective_id=0, has_side_effects=True, vmem_limit_bytes=63 * 2**20),
    )(tokens.reshape(rows), cotangent.reshape(rows), gain[None], up_weight, down_weight)
    out, gain_out, grad_up, grad_down = pl.pallas_call(
        closing_kernel,
        out_shape=(out_shape, gain_shape, grad_shape, grad_shape),
        in_specs=[anywhere] * 5,
        out_specs=(anywhere,) * 4,
        scratch_shapes=[
            pltpu.VMEM((32, D), BF16),
            pltpu.VMEM((1, D), F32),
            pltpu.VMEM((2, 16, TAIL), BF16),
            pltpu.VMEM((2, 16, TAIL), BF16),
            pltpu.VMEM((2, OWN, D), BF16),
            pltpu.SemaphoreType.DMA((12,)),
            pltpu.SemaphoreType.DMA((10,)),
        ],
        compiler_params=pltpu.CompilerParams(vmem_limit_bytes=63 * 2**20),
    )(*parts)
    return (out[None], gain_out[0], grad_up, grad_down)


def solution(mesh):
    placed = (
        P("blk", None, None),
        P("blk", None, None),
        P(),
        P(("dp", "blk"), None),
        P(("dp", "blk"), None),
    )
    return jax.shard_map(
        body,
        mesh=mesh,
        in_specs=placed,
        out_specs=(P("blk", "dp", None), P(), P(("dp", "blk"), None), P(("dp", "blk"), None)),
        check_vma=False,
    )
```
